768 devices in a mesh: dom: 96 (over z, y), sub: 8 (over x, core).
Axes of the slice: x: 4, y: 8, z: 12, core: 2. Of those that a mesh axis runs over, the one named last changes fastest.
Arguments:
- state: float32 [128, 786432], P(None, ('dom', 'sub')), may hold values from -6 to 6
- cotangent: float32 [128, 786432], P(None, ('dom', 'sub')), may hold values from -6 to 6
- velocity: float32 [3, 786432], P(None, ('dom', 'sub')), may hold values from -4 to 4
- dispersion: float32 [786432], P(('dom', 'sub')), may hold values from 0.1 to 1
- retained: float32 [128, 786432], P(None, ('dom', 'sub')), may hold values from 0 to 0.9
- kappa: float32 [12288], P(('dom', 'sub')), may hold values from 1 to 40
- elem_block: int32 [786432], P(('dom', 'sub')), may hold values from 0 to 127
- face_source: int32 [6, 786432], P(None, ('dom', 'sub')), may hold values from 0 to 8448, as said below
- send_face: int32 [6, 294912], P(None, ('dom', 'sub')), may hold values from 0 to 6144, as said below
Outputs:
- advanced: float32 [128, 786432], P(None, ('dom', 'sub'))
- adjoint: float32 [128, 786432], P(None, ('dom', 'sub'))
- rate_grad: float32 [12288], P(('dom', 'sub'))
The draws below stay inside these ranges and needn't reach their ends.
Inputs may be any that keep to these rules, and one draw needn't show every extreme that they name: `face_source`: own faces are numbered f * 1024 + e within a partition. Each own face names another own face that names it back, a slot 6144 + r * 384 + k of a used slot k of round r whose send_face entry is that very face, or the last value (outer boundary of the reach); no value but the last is named twice within a partition. `send_face`: in round r a partition lists its faces shared with the partition at dom offset o_r (same sub index) in the leading slots, the others hold 6144; slot k of round r at dom index d and slot k of round 2 * 3 - 1 - r at dom index d + o_r are the same face, and both partitions use equally many slots there. No round uses more than 384 slots, and some round of some partition uses all 384. Rounds leading outside the reach use none.
All inputs are finite; a program needn't handle non-finite values.
Results may differ from the reference program's by a relative error of at most 0.0001.
Values sent between devices are 32-bit elements; how exact they have to be, the bound alone decides.
A program may use at most 32 MiB of HBM per device.

```python
import math
import jax
import jax.numpy as jnp
import numpy as np
from jax import lax

NODE_ROWS = 128
REACH = 3
E_DEV = 1024
CAP = 384
NB_ROW = 128
ELEMS = 786432
BLOCKS = 12288
N_DOM = 96
N_SUB = 8


def partner_counts(key):
    dom_index = jnp.arange(N_DOM)[:, None]
    fullest = jax.random.randint(jax.random.fold_in(key, 7), (), 0, N_DOM - 1)
    pair_rows = []
    for distance in range(1, REACH + 1):
        least_count = CAP // 2 ** (distance + 1)
        most_count = CAP * (REACH + 1 - distance) // REACH
        drawn_counts = jax.random.randint(jax.random.fold_in(key, 10 + distance), (N_DOM, N_SUB), least_count, most_count + 1)
        if distance == 1:
            drawn_counts = jnp.where(dom_index == fullest, CAP, drawn_counts)
        drawn_counts = jnp.where(dom_index + distance < N_DOM, drawn_counts, 0)
        pair_rows.append(drawn_counts.astype(jnp.int32))
    per_round = []
    for round_number in range(2 * REACH):
        if round_number < REACH:
            distance = REACH - round_number
            shifted = jnp.concatenate([jnp.zeros((distance, N_SUB), jnp.int32), pair_rows[distance - 1][:N_DOM - distance]], axis=0)
            per_round.append(shifted)
        else:
            per_round.append(pair_rows[round_number - REACH])
    return jnp.stack(per_round, axis=-1).reshape(N_DOM * N_SUB, 2 * REACH)


def device_layout(key, counts):
    face_total = 6 * E_DEV
    rounds = 2 * REACH
    face_order = jax.random.permutation(jax.random.fold_in(key, 1), face_total).astype(jnp.int32)
    border = jax.random.randint(jax.random.fold_in(key, 2), (), face_total // 16, face_total // 8 + 1)
    round_ends = jnp.cumsum(counts)
    starts = round_ends - counts
    partner_total = round_ends[-1]
    position = jnp.arange(face_total, dtype=jnp.int32)
    round_found = jnp.sum((position[:, None] >= round_ends[None, :]).astype(jnp.int32), axis=1)
    round_safe = jnp.minimum(round_found, rounds - 1)
    slot_found = position - starts[round_safe]
    from_partner = 6 * E_DEV + round_safe * CAP + slot_found
    paired_rank = position - partner_total - border
    mate_position = jnp.where(paired_rank % 2 == 0, position + 1, position - 1)
    is_paired = (paired_rank >= 0) & (mate_position < face_total)
    from_own = face_order[jnp.clip(mate_position, 0, face_total - 1)]
    outside = 6 * E_DEV + rounds * CAP
    source_at = jnp.where(position < partner_total, from_partner, jnp.where(is_paired, from_own, outside))
    face_source = jnp.zeros((face_total,), jnp.int32).at[face_order].set(source_at.astype(jnp.int32))
    slot_index = jnp.arange(CAP, dtype=jnp.int32)[None, :]
    slot_used = slot_index < counts[:, None]
    picked = face_order[jnp.clip(starts[:, None] + slot_index, 0, face_total - 1)]
    send_list = jnp.where(slot_used, picked, face_total).astype(jnp.int32)
    return (face_source.reshape(6, E_DEV), send_list)


def interface_layout(key):
    counts = partner_counts(jax.random.fold_in(key, 3))
    devices = jnp.arange(N_DOM * N_SUB)
    device_key = jax.random.fold_in(key, 5)

    def one_device(device, device_counts):
        return device_layout(jax.random.fold_in(device_key, device), device_counts)
    sources, send_lists = jax.vmap(one_device)(devices, counts)
    sources = jnp.transpose(sources, (1, 0, 2)).reshape(6, N_DOM * N_SUB * E_DEV)
    send_lists = jnp.transpose(send_lists, (1, 0, 2)).reshape(2 * REACH, N_DOM * N_SUB * CAP)
    return (sources, send_lists)


def draw_face_source(key, part):
    return interface_layout(key)[0]


def draw_send_face(key, part):
    return interface_layout(key)[1]


def set_ends(result, key, low, high):
    index_at = [jax.random.randint(jax.random.fold_in(key, axis), (), 0, length) for axis, length in enumerate(result.shape)]
    widest = result.shape.index(max(result.shape))
    neighbour = index_at[:widest] + [(index_at[widest] + 1) % result.shape[widest]] + index_at[widest + 1:]
    return result.at[tuple(index_at)].set(low).at[tuple(neighbour)].set(high)


def steps_of(own_key, dims, cuts, least, top_value):
    def one(axis_at, shards_of):
        draws = jax.random.uniform(jax.random.fold_in(jax.random.fold_in(own_key, 6), axis_at), (shards_of,), jnp.float32, least / len(cuts), top_value / len(cuts))
        return jnp.repeat(jnp.exp(draws), dims[axis_at] // shards_of).reshape((-1,) + (1,) * (len(dims) - axis_at - 1))

    level = one(*cuts[0])
    for cut in cuts[1:]:
        level = level * one(*cut)
    return level


def centred(key, extent, spread, reach, split=(), held_as=jnp.bfloat16):
    drawn = spread * jax.random.normal(key, extent, jnp.float32)
    if split:
        drawn = drawn * steps_of(key, extent, split, -0.22, 0.18)
    return jnp.clip(drawn, -reach, reach).astype(held_as)


def setup_inputs(seed: int = 0) -> dict:
    key_list = jax.random.split(jax.random.key(seed), 10)
    state = centred(key_list[0], (NODE_ROWS, ELEMS), 1.0, 6.0, ((1, 768),), jnp.float32)
    cotangent = centred(key_list[1], (NODE_ROWS, ELEMS), 1.0, 6.0, ((1, 768),), jnp.float32)
    velocity = centred(key_list[2], (3, ELEMS), 1.0, 4.0, ((1, 768),), jnp.float32)
    dispersion = jnp.clip(jnp.exp(math.log(1.0) - 2.3025851 * jax.random.uniform(key_list[3], (ELEMS,), jnp.float32) ** steps_of(key_list[3], (ELEMS,), ((0, 768),), -0.2, 0.2)), 0.1, 1.0)
    retained = jnp.clip(0.9 * jax.random.uniform(key_list[4], (NODE_ROWS, ELEMS), jnp.float32) ** steps_of(key_list[4], (NODE_ROWS, ELEMS), ((1, 768),), -0.2, 0.2), 0.0, 0.9)
    kappa = jnp.clip(jnp.exp(math.log(40.0) - 3.6888795 * jax.random.uniform(key_list[5], (BLOCKS,), jnp.float32) ** steps_of(key_list[5], (BLOCKS,), ((0, 768),), -0.2, 0.2)), 1.0, 40.0)
    elem_block = set_ends(jax.random.randint(key_list[6], (ELEMS,), 0, NB_ROW), jax.random.fold_in(key_list[6], 1), 0, NB_ROW - 1).astype(jnp.int32)
    face_source = draw_face_source(jax.random.fold_in(key_list[9], 71), 0)
    send_face = draw_send_face(jax.random.fold_in(key_list[9], 71), 0)
    return dict(state=state, cotangent=cotangent, velocity=velocity, dispersion=dispersion, retained=retained, kappa=kappa, elem_block=elem_block, face_source=face_source, send_face=send_face)


STEP = 0.02
SECOND_SPECIES = 0.35

def nodal_operator():
    inner_point = 1.0 / np.sqrt(5.0)
    points = np.array([-1.0, -inner_point, inner_point, 1.0])
    bary_weight = np.array([1.0 / np.prod([points[j] - points[m] for m in range(4) if m != j]) for j in range(4)])
    derivative = np.zeros((4, 4))
    for i in range(4):
        for j in range(4):
            if i != j:
                derivative[i, j] = bary_weight[j] / bary_weight[i] / (points[i] - points[j])
        derivative[i, i] = -np.sum(derivative[i])
    identity = np.eye(4)
    along_i = np.kron(identity, np.kron(identity, derivative))
    along_j = np.kron(identity, np.kron(derivative, identity))
    along_k = np.kron(derivative, np.eye(16))
    second = along_i @ along_i + along_j @ along_j + along_k @ along_k
    stacked = np.concatenate([np.kron(np.eye(2), matrix) for matrix in (along_i, along_j, along_k, second)], axis=0)
    return jnp.asarray(stacked, dtype=jnp.float32)

def partner_offsets():
    return [number - REACH for number in range(REACH)] + [number + 1 for number in range(REACH)]

def face_traces(field):
    elem_count = field.shape[-1]
    node_cube = field.reshape(2, 4, 4, 4, elem_count)
    pieces = [node_cube[:, :, :, 0], node_cube[:, :, :, 3], node_cube[:, :, 0], node_cube[:, :, 3], node_cube[:, 0], node_cube[:, 3]]
    return [piece.reshape(32, elem_count) for piece in pieces]

def add_to_faces(field, face_terms):
    elem_count = field.shape[-1]
    node_cube = field.reshape(2, 4, 4, 4, elem_count)
    shaped = [face_term.reshape(2, 4, 4, elem_count) for face_term in face_terms]
    node_cube = node_cube.at[:, :, :, 0].add(shaped[0])
    node_cube = node_cube.at[:, :, :, 3].add(shaped[1])
    node_cube = node_cube.at[:, :, 0].add(shaped[2])
    node_cube = node_cube.at[:, :, 3].add(shaped[3])
    node_cube = node_cube.at[:, 0].add(shaped[4])
    node_cube = node_cube.at[:, 3].add(shaped[5])
    return node_cube.reshape(128, elem_count)

def face_weights(velocity):
    weights = []
    for face_number in range(6):
        normal_sign = 1.0 if face_number % 2 == 1 else -1.0
        weights.append(6.0 * jnp.minimum(normal_sign * velocity[face_number // 2], 0.0))
    return weights

def volume_flow(operator, field, velocity, dispersion):
    images = jnp.dot(operator, field, precision=lax.Precision.HIGHEST, preferred_element_type=jnp.float32)
    return -velocity[0] * images[0:128] - velocity[1] * images[128:256] - velocity[2] * images[256:384] + dispersion * images[384:512]

def volume_adjoint(operator, field, velocity, dispersion):
    scaled = jnp.concatenate([-velocity[0] * field, -velocity[1] * field, -velocity[2] * field, dispersion * field], axis=0)
    return jnp.dot(operator.T, scaled, precision=lax.Precision.HIGHEST, preferred_element_type=jnp.float32)

def outgoing(state, cotangent, velocity, face_source, send_face):
    elem_count = state.shape[1]
    own_rows = 6 * elem_count
    rounds, capacity = send_face.shape
    weights = face_weights(velocity)
    state_traces = face_traces(state)
    cotangent_traces = face_traces(cotangent)
    own_table = jnp.concatenate(state_traces + [jnp.zeros((32, 1), jnp.float32)], axis=1)
    send_state = own_table[:, send_face]
    pulled = jnp.concatenate([weights[face_number] * cotangent_traces[face_number] for face_number in range(6)], axis=1)
    back_rows = jnp.zeros((32, own_rows + rounds * capacity + 1), jnp.float32).at[:, face_source.reshape(-1)].add(-pulled)
    send_back = back_rows[:, own_rows:own_rows + rounds * capacity].reshape(32, rounds, capacity)
    return (send_state, send_back, (state_traces, cotangent_traces, weights, back_rows[:, :own_rows]))

def finish(operator, state, cotangent, velocity, dispersion, retained, elem_rate, face_source, send_face, local_parts, arrived_state, arrived_back):
    state_traces, cotangent_traces, weights, own_back = local_parts
    elem_count = state.shape[1]
    species_gain = jnp.where(jnp.arange(128) < 64, 1.0, SECOND_SPECIES).astype(jnp.float32)
    uptake = elem_rate[None, :] * species_gain[:, None] * (1.0 - retained)
    zero_column = jnp.zeros((32, 1), jnp.float32)
    full_table = jnp.concatenate(state_traces + [arrived_state.reshape(32, -1), zero_column], axis=1)
    outer = full_table[:, face_source.reshape(-1)]
    state_terms = [weights[face_number] * (state_traces[face_number] - outer[:, face_number * elem_count:(face_number + 1) * elem_count]) for face_number in range(6)]
    advanced = state + STEP * add_to_faces(volume_flow(operator, state, velocity, dispersion) - uptake * state, state_terms)
    back_table = jnp.concatenate([own_back, zero_column], axis=1).at[:, send_face.reshape(-1)].add(arrived_back.reshape(32, -1))
    cotangent_terms = [weights[face_number] * cotangent_traces[face_number] + back_table[:, face_number * elem_count:(face_number + 1) * elem_count] for face_number in range(6)]
    adjoint = cotangent + STEP * add_to_faces(volume_adjoint(operator, cotangent, velocity, dispersion) - uptake * cotangent, cotangent_terms)
    elem_terms = lax.optimization_barrier(jnp.sum(cotangent * species_gain[:, None] * (1.0 - retained) * state, axis=0))
    return (advanced, adjoint, elem_terms)

def from_dom_offset(array, offset):
    if offset > 0:
        return jnp.concatenate([array[offset:], jnp.zeros_like(array[:offset])], axis=0)
    return jnp.concatenate([jnp.zeros_like(array[offset:]), array[:offset]], axis=0)

def reference(state, cotangent, velocity, dispersion, retained, kappa, elem_block, face_source, send_face):
    devices = N_DOM * N_SUB
    rounds = 2 * REACH
    offsets = partner_offsets()
    operator = nodal_operator()
    state_dev = state.reshape(128, devices, E_DEV).transpose(1, 0, 2)
    cotangent_dev = cotangent.reshape(128, devices, E_DEV).transpose(1, 0, 2)
    retained_dev = retained.reshape(128, devices, E_DEV).transpose(1, 0, 2)
    velocity_dev = velocity.reshape(3, devices, E_DEV).transpose(1, 0, 2)
    dispersion_dev = dispersion.reshape(devices, E_DEV)
    block_dev = elem_block.reshape(devices, E_DEV).astype(jnp.int32)
    source_dev = face_source.reshape(6, devices, E_DEV).transpose(1, 0, 2)
    send_dev = send_face.reshape(rounds, devices, CAP).transpose(1, 0, 2)
    kappa_dev = jnp.broadcast_to(kappa.reshape(N_DOM, 1, NB_ROW), (N_DOM, N_SUB, NB_ROW)).reshape(devices, NB_ROW)
    rate_dev = jnp.take_along_axis(kappa_dev, block_dev, axis=1)

    def first_pass(inputs):
        sent = outgoing(inputs[0], inputs[1], inputs[2], inputs[3], inputs[4])
        return (sent[0], sent[1])
    sent_state, sent_back = lax.map(first_pass, (state_dev, cotangent_dev, velocity_dev, source_dev, send_dev))
    sent_state = sent_state.reshape(N_DOM, N_SUB, 32, rounds, CAP)
    sent_back = sent_back.reshape(N_DOM, N_SUB, 32, rounds, CAP)
    arrived_state = jnp.stack([from_dom_offset(sent_state[:, :, :, rounds - 1 - number], offsets[number]) for number in range(rounds)], axis=3).reshape(devices, 32, rounds, CAP)
    arrived_back = jnp.stack([from_dom_offset(sent_back[:, :, :, rounds - 1 - number], offsets[number]) for number in range(rounds)], axis=3).reshape(devices, 32, rounds, CAP)

    def second_pass(inputs):
        state_one, cotangent_one, velocity_one, dispersion_one, retained_one, rate_one, source_one, send_one, got_state, got_back = inputs
        local_parts = outgoing(state_one, cotangent_one, velocity_one, source_one, send_one)[2]
        return finish(operator, state_one, cotangent_one, velocity_one, dispersion_one, retained_one, rate_one, source_one, send_one, local_parts, got_state, got_back)
    advanced_dev, adjoint_dev, terms_dev = lax.map(second_pass, (state_dev, cotangent_dev, velocity_dev, dispersion_dev, retained_dev, rate_dev, source_dev, send_dev, arrived_state, arrived_back))
    advanced = advanced_dev.transpose(1, 0, 2).reshape(128, devices * E_DEV)
    adjoint = adjoint_dev.transpose(1, 0, 2).reshape(128, devices * E_DEV)
    terms_rows = terms_dev.reshape(N_DOM, N_SUB * E_DEV)
    blocks_rows = block_dev.reshape(N_DOM, N_SUB * E_DEV)
    sums = jax.vmap(lambda values, ids: jax.ops.segment_sum(values, ids, num_segments=NB_ROW))(terms_rows, blocks_rows)
    rate_grad = -STEP * sums.reshape(N_DOM * NB_ROW)
    return (advanced, adjoint, rate_grad)
```

```python
import functools

import jax
import jax.numpy as jnp
import numpy as np
from jax import lax
from jax.experimental import pallas as pl
from jax.experimental.pallas import tpu as pltpu
from jax.sharding import PartitionSpec as P

REACH = 3
ROUNDS = 2 * REACH
STEP = 0.02
SECOND_SPECIES = 0.35
ELEMS = 1024
FACES = 6 * ELEMS
CAP = 384
HALF = CAP // 2
TABLE = FACES + ROUNDS * CAP + 8
N_SUB = 8
BLOCKS = 128
MESH = pl.DeviceIdType.MESH
F32 = jnp.float32
BF16 = jnp.bfloat16


def nodal_matrices():
    inner_point = 1.0 / np.sqrt(5.0)
    points = np.array([-1.0, -inner_point, inner_point, 1.0])
    bary_weight = np.array(
        [1.0 / np.prod([points[j] - points[m] for m in range(4) if m != j]) for j in range(4)]
    )
    derivative = np.zeros((4, 4))
    for i in range(4):
        for j in range(4):
            if i != j:
                derivative[i, j] = bary_weight[j] / bary_weight[i] / (points[i] - points[j])
        derivative[i, i] = -np.sum(derivative[i])
    identity = np.eye(4)
    along_i = np.kron(identity, np.kron(identity, derivative))
    along_j = np.kron(identity, np.kron(derivative, identity))
    along_k = np.kron(derivative, np.eye(16))
    second = along_i @ along_i + along_j @ along_j + along_k @ along_k
    return [np.kron(np.eye(2), matrix) for matrix in (along_i, along_j, along_k, second)]


def split_constant(matrices):
    stacked = np.concatenate(matrices, axis=0).astype(np.float32)
    high = stacked.astype(BF16)
    low = (stacked - high.astype(np.float32)).astype(BF16)
    return np.concatenate([high, high, low], axis=1)


def face_rows(face):
    rows = []
    for species in range(2):
        for slow in range(4):
            for fast in range(4):
                direction, last = face // 2, 3 * (face % 2)
                if direction == 0:
                    node = last + 4 * fast + 16 * slow
                elif direction == 1:
                    node = fast + 4 * last + 16 * slow
                else:
                    node = fast + 4 * slow + 16 * last
                rows.append(species * 64 + node)
    return rows


def face_expansion():
    expand = np.zeros((128, 192), np.float32)
    for face in range(6):
        for place, row in enumerate(face_rows(face)):
            expand[row, face * 32 + place] = 1.0
    return np.concatenate([expand, expand], axis=1).astype(BF16)


def split2(x):
    high = x.astype(BF16)
    return high, (x - high.astype(F32)).astype(BF16)


def split3(x):
    high, rest = x.astype(BF16), None
    rest = x - high.astype(F32)
    middle = rest.astype(BF16)
    return high, middle, (rest - middle.astype(F32)).astype(BF16)


def iota(shape, axis):
    return lax.broadcasted_iota(jnp.int32, shape, axis)


def trace_of(ref, face, chunk):
    direction, upper = face // 2, face % 2
    if direction == 0:
        return ref[chunk, pl.ds(3 * upper, 32, stride=4), :]
    if direction == 2:
        start = 48 * upper
        return jnp.concatenate(
            [ref[chunk, pl.ds(start, 16), :], ref[chunk, pl.ds(64 + start, 16), :]], axis=0
        )
    low_half = iota((8, 128), 0) < 4
    pieces = []
    for n in range(0, 8, 2):
        if upper == 0:
            first = ref[chunk, pl.ds(16 * n, 8), :]
            second = ref[chunk, pl.ds(16 * (n + 1) - 4, 8), :]
        else:
            first = ref[chunk, pl.ds(16 * n + 12, 8), :]
            second = ref[chunk, pl.ds(16 * (n + 1) + 8, 8), :]
        pieces.append(jnp.where(low_half, first, second))
    return jnp.concatenate(pieces, axis=0)


def face_weight(velocity, face):
    normal = velocity[face // 2 : face // 2 + 1]
    return 6.0 * jnp.minimum(normal if face % 2 else -normal, 0.0)


def expand_faces(pair_rows, velocity, expansion):
    outer_parts, back_parts = [], []
    for pair in range(3):
        columns = jnp.transpose(pair_rows(pair))
        for side in range(2):
            weight = face_weight(velocity, 2 * pair + side) * (-STEP)
            outer_parts.append(columns[64 * side : 64 * side + 32] * weight)
            back_parts.append(columns[64 * side + 32 : 64 * side + 64] * STEP)
    terms = jnp.concatenate(
        [jnp.concatenate(outer_parts, axis=0), jnp.concatenate(back_parts, axis=0)], axis=1
    )
    high, low = split2(terms)
    added = jnp.dot(
        expansion, jnp.concatenate([high, low], axis=0), preferred_element_type=F32
    )
    return added[:, :128], added[:, 128:]


def exchange_kernel(
    n_dom,
    state_hbm,
    cotangent_hbm,
    velocity_hbm,
    dispersion_hbm,
    retained_hbm,
    kappa_hbm,
    block_hbm,
    source_hbm,
    send_hbm,
    forward_hbm,
    backward_hbm,
    expansion_hbm,
    advanced,
    adjoint,
    arrived_out,
    sums_out,
    state,
    cotangent,
    velocity,
    dispersion,
    retained,
    block,
    forward_op,
    backward_op,
    expansion,
    kappa_ref,
    source_index,
    send_index,
    table,
    pairs,
    outgoing,
    kappa_rows,
    sums_row,
    sums_acc,
    in_sem,
    field_sem,
    index_sem,
    send_sem,
    recv_sem,
    kappa_send,
    kappa_recv,
    sums_send,
    sums_recv,
):
    dom = lax.axis_index("dom")
    sub = lax.axis_index("sub")
    loads = {}
    for number, (name, src, dst) in enumerate(
        [
            ("velocity", velocity_hbm, velocity),
            ("kappa", kappa_hbm, kappa_ref),
            ("block", block_hbm, block),
            ("dispersion", dispersion_hbm, dispersion),
            ("forward", forward_hbm, forward_op),
            ("backward", backward_hbm, backward_op),
            ("expansion", expansion_hbm, expansion),
        ]
    ):
        loads[name] = pltpu.make_async_copy(src, dst, in_sem.at[number])
    send_loads = [
        pltpu.make_async_copy(
            send_hbm.at[number], send_index.at[pl.ds(number * CAP, CAP)], index_sem.at[number]
        )
        for number in range(ROUNDS)
    ]
    source_loads = [
        pltpu.make_async_copy(
            source_hbm.at[face],
            source_index.at[pl.ds(face * ELEMS, ELEMS)],
            index_sem.at[ROUNDS + face],
        )
        for face in range(6)
    ]

    def field_load(number, chunk):
        src, dst = ((state_hbm, state), (cotangent_hbm, cotangent), (retained_hbm, retained))[number]
        start = chunk * 128 if isinstance(chunk, int) else pl.multiple_of(chunk * 128, 128)
        return pltpu.make_async_copy(
            src.at[:, pl.ds(start, 128)], dst.at[chunk], field_sem.at[number, chunk]
        )

    loads["velocity"].start()
    loads["kappa"].start()
    for chunk in range(ELEMS // 128):
        for number in range(2):
            field_load(number, chunk).start()
    for load in send_loads:
        load.start()
    for load in source_loads:
        load.start()
    for chunk in range(ELEMS // 128):
        field_load(2, chunk).start()
    for name in ("block", "dispersion", "forward", "backward", "expansion"):
        loads[name].start()

    def dom_partner(offset):
        return lax.rem(dom + (offset + n_dom), n_dom)

    def sub_partner(turn):
        return lax.rem(sub + turn, N_SUB)

    offsets = [n - REACH if n < REACH else n - REACH + 1 for n in range(ROUNDS)]
    barrier = pltpu.get_barrier_semaphore()
    for offset in offsets:
        pl.semaphore_signal(
            barrier, inc=1, device_id={"dom": dom_partner(offset)}, device_id_type=MESH
        )
    for turn in range(1, N_SUB):
        pl.semaphore_signal(
            barrier, inc=1, device_id={"sub": sub_partner(turn)}, device_id_type=MESH
        )

    zero_tile = jnp.zeros((8, 128), F32)

    def clear(step, carry):
        table[pl.ds(pl.multiple_of(FACES + step * 8, 8), 8), :] = zero_tile
        return carry

    lax.fori_loop(0, (TABLE - FACES) // 8, clear, 0, unroll=17)

    lane_row = iota((1, 128), 1)
    own_row = jnp.zeros((1, 128), F32)
    loads["kappa"].wait()
    for place in range(16):
        own_row = jnp.where(lane_row == sub * 16 + place, kappa_ref[place], own_row)
    kappa_rows[0] = own_row

    loads["velocity"].wait()
    low_lanes = iota((128, 128), 1) < 64

    def build(chunk, carry):
        field_load(0, chunk).wait()
        field_load(1, chunk).wait()
        start = pl.multiple_of(chunk * 128, 128)
        cols = pl.ds(start, 128)
        speeds = velocity[:, cols]
        for pair in range(3):
            parts = []
            for face in (2 * pair, 2 * pair + 1):
                parts.append(trace_of(state, face, chunk))
                parts.append(trace_of(cotangent, face, chunk) * (-face_weight(speeds, face)))
            rows = jnp.transpose(jnp.concatenate(parts, axis=0))
            turned = pltpu.roll(rows, 64, 1)
            table[pl.ds(pl.multiple_of(2 * pair * ELEMS + start, 128), 128), :] = jnp.where(
                low_lanes, rows, turned
            )
            table[pl.ds(pl.multiple_of((2 * pair + 1) * ELEMS + start, 128), 128), :] = jnp.where(
                low_lanes, turned, rows
            )
        return carry

    lax.fori_loop(0, ELEMS // 128, build, 0)
    low_row = iota((1, 128), 1) < 64

    for load in send_loads:
        load.wait()
    pl.semaphore_wait(barrier, ROUNDS + N_SUB - 1)

    kappa_copies = [
        pltpu.make_async_remote_copy(
            src_ref=kappa_rows.at[0],
            dst_ref=kappa_rows.at[turn],
            send_sem=kappa_send.at[turn],
            recv_sem=kappa_recv.at[turn],
            device_id={"sub": sub_partner(turn)},
            device_id_type=MESH,
        )
        for turn in range(1, N_SUB)
    ]
    for copy in kappa_copies:
        copy.start()

    group = 32
    round_copies = []
    for number in (0, 5, 1, 4, 2, 3):

        def gather(step, carry, number=number):
            base = step * group
            values = []
            for place in range(group):
                first = send_index[number * CAP + base + place]
                second = send_index[number * CAP + HALF + base + place]
                values.append(
                    jnp.where(low_row, table[pl.ds(first, 1), :], table[pl.ds(second, 1), :])
                )
            for place in range(group):
                outgoing[number, pl.ds(base + place, 1), :] = values[place]
            return carry

        lax.fori_loop(0, HALF // group, gather, 0)
        copy = pltpu.make_async_remote_copy(
            src_ref=outgoing.at[number],
            dst_ref=arrived_out.at[ROUNDS - 1 - number],
            send_sem=send_sem.at[number],
            recv_sem=recv_sem.at[ROUNDS - 1 - number],
            device_id={"dom": dom_partner(offsets[number])},
            device_id_type=MESH,
        )
        copy.start()
        round_copies.append(copy)

    for copy in kappa_copies:
        copy.wait_recv()
    slab = kappa_rows[0]
    for turn in range(1, N_SUB):
        slab = slab + kappa_rows[turn]
    slab_parts = jnp.concatenate(
        list(split3(slab)) + [jnp.zeros((13, 128), BF16)], axis=0
    )
    for name in ("block", "dispersion", "forward", "backward"):
        loads[name].wait()
    for chunk in range(ELEMS // 128):
        field_load(2, chunk).wait()
    sums_acc[...] = jnp.zeros_like(sums_acc)

    width = 256
    sublane = iota((8, width), 0)

    def volume(chunk, carry):
        start = pl.multiple_of(chunk * width, width)
        cols = pl.ds(start, width)
        hits = (iota((BLOCKS, width), 0) == block[:, cols]).astype(F32).astype(BF16)
        rates = jnp.dot(slab_parts, hits, preferred_element_type=F32)
        elem_rate = (rates[0:1] + rates[1:2]) + rates[2:3]
        speeds = velocity[:, cols]
        spread = dispersion[:, cols] * STEP

        def two_chunks(ref):
            return jnp.concatenate([ref[2 * chunk], ref[2 * chunk + 1]], axis=1)

        field = two_chunks(state)
        dual = two_chunks(cotangent)
        weights = [face_weight(speeds, face) for face in range(6)]
        along_i = jnp.where(
            sublane % 4 == 0, weights[0], jnp.where(sublane % 4 == 3, weights[1], 0.0)
        )
        by_j = [
            along_i + jnp.where(sublane < 4, weights[2], 0.0),
            along_i + jnp.where(sublane >= 4, weights[3], 0.0),
        ]
        tiles = [by_j[0] + weights[4], by_j[1] + weights[4]]
        tiles += [by_j[0], by_j[1], by_j[0], by_j[1]]
        tiles += [by_j[0] + weights[5], by_j[1] + weights[5]]
        face_part = jnp.concatenate(tiles + tiles, axis=0)
        gain = jnp.where(iota((128, width), 0) < 64, 1.0, SECOND_SPECIES)
        free = gain * (1.0 - two_chunks(retained))
        factor = 1.0 + STEP * (face_part - elem_rate * free)
        terms = jnp.sum(free * dual * field, axis=0, keepdims=True)
        term_parts = jnp.concatenate(
            list(split3(terms)) + [jnp.zeros((13, width), BF16)], axis=0
        )
        sums_acc[...] += lax.dot_general(
            term_parts, hits, (((1,), (1,)), ((), ())), preferred_element_type=F32
        )
        for values, operator, target in (
            (field, forward_op, advanced),
            (dual, backward_op, adjoint),
        ):
            high, low = split2(values)
            images = jnp.dot(
                operator[...],
                jnp.concatenate([high, low, high], axis=0),
                preferred_element_type=F32,
            )
            target[:, cols] = (
                factor * values
                - (STEP * speeds[0:1]) * images[0:128]
                - (STEP * speeds[1:2]) * images[128:256]
                - (STEP * speeds[2:3]) * images[256:384]
                + spread * images[384:512]
            )
        return carry

    lax.fori_loop(0, ELEMS // width, volume, 0)
    sums_row[...] = (sums_acc[0:1] + sums_acc[1:2]) + sums_acc[2:3]

    sums_out[0] = sums_row[...]
    sums_copies = [
        pltpu.make_async_remote_copy(
            src_ref=sums_row,
            dst_ref=sums_out.at[turn],
            send_sem=sums_send.at[turn],
            recv_sem=sums_recv.at[turn],
            device_id={"sub": sub_partner(turn)},
            device_id_type=MESH,
        )
        for turn in range(1, N_SUB)
    ]
    for copy in sums_copies:
        copy.start()

    for load in source_loads:
        load.wait()
    for pair in range(3):

        def pick(step, carry, pair=pair):
            base = step * group
            values = []
            for place in range(group):
                first = source_index[2 * pair * ELEMS + base + place]
                second = source_index[(2 * pair + 1) * ELEMS + base + place]
                values.append(
                    jnp.where(low_row, table[pl.ds(first, 1), :], table[pl.ds(second, 1), :])
                )
            for place in range(group):
                pairs[pl.ds(pair * ELEMS + base + place, 1), :] = values[place]
            return carry

        lax.fori_loop(0, ELEMS // group, pick, 0)

    loads["expansion"].wait()

    def close(chunk, carry):
        start = pl.multiple_of(chunk * 128, 128)
        cols = pl.ds(start, 128)
        added = expand_faces(
            lambda pair: pairs[pl.ds(pl.multiple_of(pair * ELEMS + start, 128), 128), :],
            velocity[:, cols],
            expansion[...],
        )
        advanced[:, cols] += added[0]
        adjoint[:, cols] += added[1]
        return carry

    lax.fori_loop(0, ELEMS // 128, close, 0)
    for copy in kappa_copies:
        copy.wait_send()
    for copy in sums_copies:
        copy.wait()
    for copy in round_copies:
        copy.wait()


def merge_kernel(
    part_advanced,
    part_adjoint,
    arrived,
    sums,
    velocity_hbm,
    send_hbm,
    expansion_hbm,
    advanced_out,
    adjoint_out,
    grad_out,
    advanced,
    adjoint,
    velocity,
    expansion,
    send_index,
    rows,
    spread,
    in_sem,
    index_sem,
    out_sem,
):
    sub = lax.axis_index("sub")
    loads = [
        pltpu.make_async_copy(src, dst, in_sem.at[number])
        for number, (src, dst) in enumerate(
            [
                (velocity_hbm, velocity),
                (expansion_hbm, expansion),
            ]
        )
    ]
    index_loads = [
        pltpu.make_async_copy(
            send_hbm.at[number], send_index.at[pl.ds(number * CAP, CAP)], index_sem.at[number]
        )
        for number in range(ROUNDS)
    ]
    for load in index_loads:
        load.start()
    for load in loads:
        load.start()
    zero_tile = jnp.zeros((8, 128), F32)

    def clear(step, carry):
        for place in range(16):
            spread[pl.ds(pl.multiple_of(step * 128 + place * 8, 8), 8), :] = zero_tile
        return carry

    lax.fori_loop(0, FACES // 128, clear, 0)
    low_lanes = iota((HALF, 128), 1) < 64
    for number in range(ROUNDS):
        values = arrived[number]
        turned = pltpu.roll(values, 64, 1)
        rows[pl.ds(number * CAP, HALF), :] = jnp.where(low_lanes, values, turned)
        rows[pl.ds(number * CAP + HALF, HALF), :] = jnp.where(low_lanes, turned, values)
    for load in index_loads:
        load.wait()
    group = 64

    def scatter(step, carry):
        base = step * group
        values = [rows[pl.ds(base + place, 1), :] for place in range(group)]
        for place in range(group):
            spread[pl.ds(send_index[base + place], 1), :] = values[place]
        return carry

    lax.fori_loop(0, ROUNDS * CAP // group, scatter, 0)
    for load in loads:
        load.wait()
    total = jnp.zeros((1, 128), F32)
    for turn in range(N_SUB):
        total = total + sums[turn]
    total = pltpu.roll(total, 128 - sub * 16, 1)
    grad_out[...] = -STEP * total[:, :16]
    low_part = iota((128, 128), 1) < 64

    def results(chunk):
        cols = pl.ds(pl.multiple_of(chunk * 128, 128), 128)
        return [
            pltpu.make_async_copy(
                advanced.at[:, cols], advanced_out.at[:, cols], out_sem.at[0, chunk]
            ),
            pltpu.make_async_copy(
                adjoint.at[:, cols], adjoint_out.at[:, cols], out_sem.at[1, chunk]
            ),
        ]

    def close(chunk, carry):
        start = pl.multiple_of(chunk * 128, 128)
        cols = pl.ds(start, 128)

        def pair_rows(pair):
            first = spread[pl.ds(pl.multiple_of(2 * pair * ELEMS + start, 128), 128), :]
            second = spread[pl.ds(pl.multiple_of((2 * pair + 1) * ELEMS + start, 128), 128), :]
            return jnp.where(low_part, first, second)

        added = expand_faces(pair_rows, velocity[:, cols], expansion[...])
        advanced[:, cols] = part_advanced[:, cols] + added[0]
        adjoint[:, cols] = part_adjoint[:, cols] + added[1]
        for copy in results(chunk):
            copy.start()
        return carry

    lax.fori_loop(0, ELEMS // 128, close, 0)

    def finish(chunk, carry):
        for copy in results(chunk):
            copy.wait()
        return carry

    lax.fori_loop(0, ELEMS // 128, finish, 0)


def solution(mesh):
    n_dom = mesh.shape["dom"]
    matrices = nodal_matrices()
    forward_np = split_constant(matrices)
    backward_np = split_constant([matrix.T for matrix in matrices])
    expansion_np = face_expansion()
    in_hbm = pl.BlockSpec(memory_space=pltpu.HBM)
    in_vmem = pl.BlockSpec(memory_space=pltpu.VMEM)
    dma = pltpu.SemaphoreType.DMA
    field = jax.ShapeDtypeStruct((128, ELEMS), F32)

    def shards(
        state, cotangent, velocity, dispersion, retained, kappa, elem_block, face_source, send_face
    ):
        kept = functools.partial(pltpu.with_memory_space_constraint, memory_space=pltpu.HBM)
        forward_op = kept(jnp.asarray(forward_np))
        backward_op = kept(jnp.asarray(backward_np))
        expansion = kept(jnp.asarray(expansion_np))
        state, cotangent, velocity, retained = map(kept, (state, cotangent, velocity, retained))
        face_source, send_face, kappa = map(kept, (face_source, send_face, kappa))
        dispersion = kept(dispersion.reshape(1, ELEMS))
        elem_block = kept(elem_block.reshape(1, ELEMS))
        part_advanced, part_adjoint, arrived, sums = pl.pallas_call(
            functools.partial(exchange_kernel, n_dom),
            out_shape=(
                field,
                field,
                jax.ShapeDtypeStruct((ROUNDS, HALF, 128), F32),
                jax.ShapeDtypeStruct((N_SUB, 1, 128), F32),
            ),
            in_specs=[in_hbm] * 12,
            out_specs=(in_vmem,) * 4,
            scratch_shapes=[
                pltpu.VMEM((ELEMS // 128, 128, 128), F32),
                pltpu.VMEM((ELEMS // 128, 128, 128), F32),
                pltpu.VMEM((3, ELEMS), F32),
                pltpu.VMEM((1, ELEMS), F32),
                pltpu.VMEM((ELEMS // 128, 128, 128), F32),
                pltpu.VMEM((1, ELEMS), jnp.int32),
                pltpu.VMEM((512, 384), BF16),
                pltpu.VMEM((512, 384), BF16),
                pltpu.VMEM((128, 384), BF16),
                pltpu.SMEM((16,), F32),
                pltpu.SMEM((FACES,), jnp.int32),
                pltpu.SMEM((ROUNDS * CAP,), jnp.int32),
                pltpu.VMEM((TABLE, 128), F32),
                pltpu.VMEM((3 * ELEMS, 128), F32),
                pltpu.VMEM((ROUNDS, HALF, 128), F32),
                pltpu.VMEM((N_SUB, 1, 128), F32),
                pltpu.VMEM((1, 128), F32),
                pltpu.VMEM((16, 128), F32),
                dma((7,)),
                dma((3, ELEMS // 128)),
                dma((ROUNDS + 6,)),
                dma((ROUNDS,)),
                dma((ROUNDS,)),
                dma((N_SUB,)),
                dma((N_SUB,)),
                dma((N_SUB,)),
                dma((N_SUB,)),
            ],
            compiler_params=pltpu.CompilerParams(
                collective_id=0, has_side_effects=True, vmem_limit_bytes=40 << 20
            ),
            name="exchange",
        )(
            state,
            cotangent,
            velocity,
            dispersion,
            retained,
            kappa,
            elem_block,
            face_source,
            send_face,
            forward_op,
            backward_op,
            expansion,
        )
        advanced, adjoint, grad = pl.pallas_call(
            merge_kernel,
            out_shape=(field, field, jax.ShapeDtypeStruct((1, 16), F32)),
            in_specs=[in_vmem] * 4 + [in_hbm] * 3,
            out_specs=(in_hbm, in_hbm, in_vmem),
            scratch_shapes=[
                pltpu.VMEM((128, ELEMS), F32),
                pltpu.VMEM((128, ELEMS), F32),
                pltpu.VMEM((3, ELEMS), F32),
                pltpu.VMEM((128, 384), BF16),
                pltpu.SMEM((ROUNDS * CAP,), jnp.int32),
                pltpu.VMEM((ROUNDS * CAP, 128), F32),
                pltpu.VMEM((FACES + 8, 128), F32),
                dma((2,)),
                dma((ROUNDS,)),
                dma((2, ELEMS // 128)),
            ],
            compiler_params=pltpu.CompilerParams(vmem_limit_bytes=40 << 20),
            name="merge",
        )(part_advanced, part_adjoint, arrived, sums, velocity, send_face, expansion)
        return advanced, adjoint, grad.reshape(16)

    wide = P(None, ("dom", "sub"))
    flat = P(("dom", "sub"))
    return jax.shard_map(
        shards,
        mesh=mesh,
        in_specs=(wide, wide, wide, flat, wide, flat, flat, wide, wide),
        out_specs=(wide, wide, flat),
        check_vma=False,
    )
```

```python
import functools

import jax
import jax.numpy as jnp
import numpy as np
from jax import lax
from jax.experimental import pallas as pl
from jax.experimental.pallas import tpu as pltpu
from jax.sharding import PartitionSpec as P

REACH = 3
ROUNDS = 2 * REACH
STEP = 0.02
SECOND_SPECIES = 0.35
ELEMS = 1024
FACES = 6 * ELEMS
CAP = 384
HALF = CAP // 2
TABLE = FACES + ROUNDS * CAP + 8
N_SUB = 8
BLOCKS = 128
UNROLL_BUILD = 1
UNROLL_CLOSE = 8
MESH = pl.DeviceIdType.MESH
F32 = jnp.float32
BF16 = jnp.bfloat16


def nodal_matrices():
    inner_point = 1.0 / np.sqrt(5.0)
    points = np.array([-1.0, -inner_point, inner_point, 1.0])
    bary_weight = np.array(
        [1.0 / np.prod([points[j] - points[m] for m in range(4) if m != j]) for j in range(4)]
    )
    derivative = np.zeros((4, 4))
    for i in range(4):
        for j in range(4):
            if i != j:
                derivative[i, j] = bary_weight[j] / bary_weight[i] / (points[i] - points[j])
        derivative[i, i] = -np.sum(derivative[i])
    identity = np.eye(4)
    along_i = np.kron(identity, np.kron(identity, derivative))
    along_j = np.kron(identity, np.kron(derivative, identity))
    along_k = np.kron(derivative, np.eye(16))
    second = along_i @ along_i + along_j @ along_j + along_k @ along_k
    return [np.kron(np.eye(2), matrix) for matrix in (along_i, along_j, along_k, second)]


def split_constant(matrices):
    stacked = np.concatenate(matrices, axis=0).astype(np.float32)
    high = stacked.astype(BF16)
    low = (stacked - high.astype(np.float32)).astype(BF16)
    return np.concatenate([high, high, low], axis=1)


def face_rows(face):
    rows = []
    for species in range(2):
        for slow in range(4):
            for fast in range(4):
                direction, last = face // 2, 3 * (face % 2)
                if direction == 0:
                    node = last + 4 * fast + 16 * slow
                elif direction == 1:
                    node = fast + 4 * last + 16 * slow
                else:
                    node = fast + 4 * slow + 16 * last
                rows.append(species * 64 + node)
    return rows


def face_expansion():
    expand = np.zeros((128, 192), np.float32)
    for face in range(6):
        for place, row in enumerate(face_rows(face)):
            expand[row, face * 32 + place] = 1.0
    return np.concatenate([expand, expand], axis=1).astype(BF16)


def split2(x):
    high = x.astype(BF16)
    return high, (x - high.astype(F32)).astype(BF16)


def split3(x):
    high, rest = x.astype(BF16), None
    rest = x - high.astype(F32)
    middle = rest.astype(BF16)
    return high, middle, (rest - middle.astype(F32)).astype(BF16)


def iota(shape, axis):
    return lax.broadcasted_iota(jnp.int32, shape, axis)


def trace_of(ref, face, chunk):
    direction, upper = face // 2, face % 2
    if direction == 0:
        return ref[chunk, pl.ds(3 * upper, 32, stride=4), :]
    if direction == 2:
        start = 48 * upper
        return jnp.concatenate(
            [ref[chunk, pl.ds(start, 16), :], ref[chunk, pl.ds(64 + start, 16), :]], axis=0
        )
    low_half = iota((8, 128), 0) < 4
    pieces = []
    for n in range(0, 8, 2):
        if upper == 0:
            first = ref[chunk, pl.ds(16 * n, 8), :]
            second = ref[chunk, pl.ds(16 * (n + 1) - 4, 8), :]
        else:
            first = ref[chunk, pl.ds(16 * n + 12, 8), :]
            second = ref[chunk, pl.ds(16 * (n + 1) + 8, 8), :]
        pieces.append(jnp.where(low_half, first, second))
    return jnp.concatenate(pieces, axis=0)


def face_weight(velocity, face):
    normal = velocity[face // 2 : face // 2 + 1]
    return 6.0 * jnp.minimum(normal if face % 2 else -normal, 0.0)


def expand_faces(pair_rows, velocity, expansion):
    outer_parts, back_parts = [], []
    for pair in range(3):
        columns = jnp.transpose(pair_rows(pair))
        for side in range(2):
            weight = face_weight(velocity, 2 * pair + side) * (-STEP)
            outer_parts.append(columns[64 * side : 64 * side + 32] * weight)
            back_parts.append(columns[64 * side + 32 : 64 * side + 64] * STEP)
    terms = jnp.concatenate(
        [jnp.concatenate(outer_parts, axis=0), jnp.concatenate(back_parts, axis=0)], axis=1
    )
    high, low = split2(terms)
    added = jnp.dot(
        expansion, jnp.concatenate([high, low], axis=0), preferred_element_type=F32
    )
    return added[:, :128], added[:, 128:]


def exchange_kernel(
    n_dom,
    state_hbm,
    cotangent_hbm,
    velocity_hbm,
    dispersion_hbm,
    retained_hbm,
    kappa_hbm,
    block_hbm,
    source_hbm,
    send_hbm,
    forward_hbm,
    backward_hbm,
    advanced,
    adjoint,
    arrived_out,
    sums_out,
    outer_rows,
    state,
    cotangent,
    velocity,
    dispersion,
    retained,
    block,
    forward_op,
    backward_op,
    kappa_ref,
    source_index,
    send_index,
    table,
    outgoing,
    kappa_rows,
    sums_row,
    sums_acc,
    in_sem,
    field_sem,
    index_sem,
    send_sem,
    recv_sem,
    kappa_send,
    kappa_recv,
    sums_send,
    sums_recv,
):
    dom = lax.axis_index("dom")
    sub = lax.axis_index("sub")
    loads = {}
    for number, (name, src, dst) in enumerate(
        [
            ("velocity", velocity_hbm, velocity),
            ("kappa", kappa_hbm, kappa_ref),
            ("block", block_hbm, block),
            ("dispersion", dispersion_hbm, dispersion),
            ("forward", forward_hbm, forward_op),
            ("backward", backward_hbm, backward_op),
        ]
    ):
        loads[name] = pltpu.make_async_copy(src, dst, in_sem.at[number])
    send_loads = [
        pltpu.make_async_copy(
            send_hbm.at[number], send_index.at[pl.ds(number * CAP, CAP)], index_sem.at[number]
        )
        for number in range(ROUNDS)
    ]
    source_loads = [
        pltpu.make_async_copy(
            source_hbm.at[face],
            source_index.at[pl.ds(face * ELEMS, ELEMS)],
            index_sem.at[ROUNDS + face],
        )
        for face in range(6)
    ]

    def field_load(number, chunk):
        src, dst = ((state_hbm, state), (cotangent_hbm, cotangent), (retained_hbm, retained))[number]
        start = chunk * 128 if isinstance(chunk, int) else pl.multiple_of(chunk * 128, 128)
        return pltpu.make_async_copy(
            src.at[:, pl.ds(start, 128)], dst.at[chunk], field_sem.at[number, chunk]
        )

    loads["velocity"].start()
    for chunk in range(ELEMS // 128):
        for number in range(2):
            field_load(number, chunk).start()

    def dom_partner(offset):
        return dom + offset

    def has_partner(offset):
        return dom >= -offset if offset < 0 else dom < n_dom - offset

    def sub_partner(turn):
        return lax.rem(sub + turn, N_SUB)

    offsets = [n - REACH if n < REACH else n - REACH + 1 for n in range(ROUNDS)]
    barrier = pltpu.get_barrier_semaphore()
    partner_count = N_SUB - 1
    for offset in offsets:
        partner_count = partner_count + has_partner(offset).astype(jnp.int32)

        @pl.when(has_partner(offset))
        def _(offset=offset):
            pl.semaphore_signal(
                barrier, inc=1, device_id={"dom": dom_partner(offset)}, device_id_type=MESH
            )

    for turn in range(1, N_SUB):
        pl.semaphore_signal(
            barrier, inc=1, device_id={"sub": sub_partner(turn)}, device_id_type=MESH
        )

    for load in send_loads:
        load.start()
    loads["kappa"].start()

    zero_tile = jnp.zeros((8, 128), F32)

    def clear(step, carry):
        table[pl.ds(pl.multiple_of(FACES + step * 8, 8), 8), :] = zero_tile
        return carry

    lax.fori_loop(0, (TABLE - FACES) // 8, clear, 0, unroll=17)

    loads["velocity"].wait()
    low_lanes = iota((128, 128), 1) < 64

    def build(chunk, carry):
        field_load(0, chunk).wait()
        field_load(1, chunk).wait()
        start = pl.multiple_of(chunk * 128, 128)
        cols = pl.ds(start, 128)
        speeds = velocity[:, cols]
        for pair in range(3):
            parts = []
            for face in (2 * pair, 2 * pair + 1):
                parts.append(trace_of(state, face, chunk))
                parts.append(trace_of(cotangent, face, chunk) * (-face_weight(speeds, face)))
            rows = jnp.transpose(jnp.concatenate(parts, axis=0))
            turned = pltpu.roll(rows, 64, 1)
            table[pl.ds(pl.multiple_of(2 * pair * ELEMS + start, 128), 128), :] = jnp.where(
                low_lanes, rows, turned
            )
            table[pl.ds(pl.multiple_of((2 * pair + 1) * ELEMS + start, 128), 128), :] = jnp.where(
                low_lanes, turned, rows
            )
        return carry

    lax.fori_loop(0, ELEMS // 128, build, 0, unroll=UNROLL_BUILD)
    low_row = iota((1, 128), 1) < 64

    for load in send_loads:
        load.wait()
    pl.semaphore_wait(barrier, partner_count)

    group = 32
    lane_row = iota((1, 128), 1)
    own_row = jnp.zeros((1, 128), F32)
    loads["kappa"].wait()
    for place in range(16):
        own_row = jnp.where(lane_row == sub * 16 + place, kappa_ref[place], own_row)
    kappa_rows[0] = own_row

    kappa_copies = [
        pltpu.make_async_remote_copy(
            src_ref=kappa_rows.at[0],
            dst_ref=kappa_rows.at[turn],
            send_sem=kappa_send.at[turn],
            recv_sem=kappa_recv.at[turn],
            device_id={"sub": sub_partner(turn)},
            device_id_type=MESH,
        )
        for turn in range(1, N_SUB)
    ]

    round_copies = []
    round_order = (0, 5, 1, 4, 2, 3)
    for turn, number in enumerate(round_order):

        def gather(step, carry, number=number):
            base = step * group
            values = []
            for place in range(group):
                first = send_index[number * CAP + base + place]
                second = send_index[number * CAP + HALF + base + place]
                values.append(
                    jnp.where(low_row, table[pl.ds(first, 1), :], table[pl.ds(second, 1), :])
                )
            for place in range(group):
                outgoing[number, pl.ds(base + place, 1), :] = values[place]
            return carry

        copy = pltpu.make_async_remote_copy(
            src_ref=outgoing.at[number],
            dst_ref=arrived_out.at[ROUNDS - 1 - number],
            send_sem=send_sem.at[number],
            recv_sem=recv_sem.at[ROUNDS - 1 - number],
            device_id={"dom": dom_partner(offsets[number])},
            device_id_type=MESH,
        )

        @pl.when(has_partner(offsets[number]))
        def _(gather=gather, copy=copy):
            lax.fori_loop(0, HALF // group, gather, 0)
            copy.start()

        round_copies.append(copy)
        if turn == 1:
            for copy in kappa_copies:
                copy.start()
            loads["block"].start()
            for chunk in range(ELEMS // 128):
                field_load(2, chunk).start()
        if turn == 3:
            for load in source_loads:
                load.start()
            for name in ("dispersion", "forward", "backward"):
                loads[name].start()

    width = 256
    sublane = iota((8, width), 0)

    def two_chunks(ref, chunk):
        return jnp.concatenate([ref[2 * chunk], ref[2 * chunk + 1]], axis=1)

    def free_sites(chunk):
        gain = jnp.where(iota((128, width), 0) < 64, 1.0, SECOND_SPECIES)
        return gain * (1.0 - two_chunks(retained, chunk))

    def block_hits(cols):
        return (iota((BLOCKS, width), 0) == block[:, cols]).astype(F32).astype(BF16)

    loads["block"].wait()
    for chunk in range(ELEMS // 128):
        field_load(2, chunk).wait()
    sums_acc[...] = jnp.zeros_like(sums_acc)

    def block_sums(chunk, carry):
        cols = pl.ds(pl.multiple_of(chunk * width, width), width)
        product = free_sites(chunk) * two_chunks(cotangent, chunk) * two_chunks(state, chunk)
        terms = jnp.sum(product, axis=0, keepdims=True)
        term_parts = jnp.concatenate(
            list(split3(terms)) + [jnp.zeros((13, width), BF16)], axis=0
        )
        sums_acc[...] += lax.dot_general(
            term_parts, block_hits(cols), (((1,), (1,)), ((), ())), preferred_element_type=F32
        )
        return carry

    lax.fori_loop(0, ELEMS // width, block_sums, 0)
    sums_row[...] = (sums_acc[0:1] + sums_acc[1:2]) + sums_acc[2:3]

    sums_out[0] = sums_row[...]
    sums_copies = [
        pltpu.make_async_remote_copy(
            src_ref=sums_row,
            dst_ref=sums_out.at[turn],
            send_sem=sums_send.at[turn],
            recv_sem=sums_recv.at[turn],
            device_id={"sub": sub_partner(turn)},
            device_id_type=MESH,
        )
        for turn in range(1, N_SUB)
    ]
    for copy in sums_copies:
        copy.start()

    for load in source_loads:
        load.wait()

    def pick(step, carry):
        base = step * (2 * group)
        values = [
            table[pl.ds(source_index[base + place], 1), :] for place in range(2 * group)
        ]
        for place in range(2 * group):
            outer_rows[pl.ds(base + place, 1), :] = values[place]
        return carry

    lax.fori_loop(0, FACES // (2 * group), pick, 0)

    for copy in kappa_copies:
        copy.wait_recv()
    slab = kappa_rows[0]
    for turn in range(1, N_SUB):
        slab = slab + kappa_rows[turn]
    slab_parts = jnp.concatenate(
        list(split3(slab)) + [jnp.zeros((13, 128), BF16)], axis=0
    )
    for name in ("dispersion", "forward", "backward"):
        loads[name].wait()

    def volume(chunk, carry):
        start = pl.multiple_of(chunk * width, width)
        cols = pl.ds(start, width)
        rates = jnp.dot(slab_parts, block_hits(cols), preferred_element_type=F32)
        elem_rate = (rates[0:1] + rates[1:2]) + rates[2:3]
        speeds = velocity[:, cols]
        spread = dispersion[:, cols] * STEP

        field = two_chunks(state, chunk)
        dual = two_chunks(cotangent, chunk)
        weights = [face_weight(speeds, face) for face in range(6)]
        along_i = jnp.where(
            sublane % 4 == 0, weights[0], jnp.where(sublane % 4 == 3, weights[1], 0.0)
        )
        by_j = [
            along_i + jnp.where(sublane < 4, weights[2], 0.0),
            along_i + jnp.where(sublane >= 4, weights[3], 0.0),
        ]
        tiles = [by_j[0] + weights[4], by_j[1] + weights[4]]
        tiles += [by_j[0], by_j[1], by_j[0], by_j[1]]
        tiles += [by_j[0] + weights[5], by_j[1] + weights[5]]
        face_part = jnp.concatenate(tiles + tiles, axis=0)
        free = free_sites(chunk)
        factor = 1.0 + STEP * (face_part - elem_rate * free)
        for values, operator, target in (
            (field, forward_op, advanced),
            (dual, backward_op, adjoint),
        ):
            high, low = split2(values)
            images = jnp.dot(
                operator[...],
                jnp.concatenate([high, low, high], axis=0),
                preferred_element_type=F32,
            )
            target[:, cols] = (
                factor * values
                - (STEP * speeds[0:1]) * images[0:128]
                - (STEP * speeds[1:2]) * images[128:256]
                - (STEP * speeds[2:3]) * images[256:384]
                + spread * images[384:512]
            )
        return carry

    lax.fori_loop(0, ELEMS // width, volume, 0)
    for copy in kappa_copies:
        copy.wait_send()
    for copy in sums_copies:
        copy.wait()
    for number, copy in zip(round_order, round_copies):
        pl.when(has_partner(offsets[number]))(copy.wait_send)
        pl.when(has_partner(offsets[ROUNDS - 1 - number]))(copy.wait_recv)


def merge_kernel(
    part_advanced,
    part_adjoint,
    arrived,
    sums,
    outer_rows,
    velocity_hbm,
    send_hbm,
    expansion_hbm,
    advanced_out,
    adjoint_out,
    grad_out,
    spread,
    advanced,
    adjoint,
    velocity,
    expansion,
    send_index,
    rows,
    in_sem,
    index_sem,
    out_sem,
):
    del outer_rows
    sub = lax.axis_index("sub")
    loads = [
        pltpu.make_async_copy(src, dst, in_sem.at[number])
        for number, (src, dst) in enumerate(
            [
                (velocity_hbm, velocity),
                (expansion_hbm, expansion),
            ]
        )
    ]
    index_loads = [
        pltpu.make_async_copy(
            send_hbm.at[number], send_index.at[pl.ds(number * CAP, CAP)], index_sem.at[number]
        )
        for number in range(ROUNDS)
    ]
    for load in index_loads:
        load.start()
    for load in loads:
        load.start()
    low_lanes = iota((HALF, 128), 1) < 64
    for number in range(ROUNDS):
        values = arrived[number]
        turned = pltpu.roll(values, 64, 1)
        rows[pl.ds(number * CAP, HALF), :] = jnp.where(low_lanes, values, turned)
        rows[pl.ds(number * CAP + HALF, HALF), :] = jnp.where(low_lanes, turned, values)
    for load in index_loads:
        load.wait()
    group = 64

    def scatter(step, carry):
        base = step * group
        values = [rows[pl.ds(base + place, 1), :] for place in range(group)]
        for place in range(group):
            spread[pl.ds(send_index[base + place], 1), :] = values[place]
        return carry

    lax.fori_loop(0, ROUNDS * CAP // group, scatter, 0)
    for load in loads:
        load.wait()
    total = jnp.zeros((1, 128), F32)
    for turn in range(N_SUB):
        total = total + sums[turn]
    total = pltpu.roll(total, 128 - sub * 16, 1)
    grad_out[...] = -STEP * total[:, :16]
    low_part = iota((128, 128), 1) < 64

    def results(chunk):
        cols = pl.ds(pl.multiple_of(chunk * 128, 128), 128)
        return [
            pltpu.make_async_copy(
                advanced.at[:, cols], advanced_out.at[:, cols], out_sem.at[0, chunk]
            ),
            pltpu.make_async_copy(
                adjoint.at[:, cols], adjoint_out.at[:, cols], out_sem.at[1, chunk]
            ),
        ]

    def close(chunk, carry):
        start = pl.multiple_of(chunk * 128, 128)
        cols = pl.ds(start, 128)

        def pair_rows(pair):
            first = spread[pl.ds(pl.multiple_of(2 * pair * ELEMS + start, 128), 128), :]
            second = spread[pl.ds(pl.multiple_of((2 * pair + 1) * ELEMS + start, 128), 128), :]
            return jnp.where(low_part, first, second)

        added = expand_faces(pair_rows, velocity[:, cols], expansion[...])
        advanced[:, cols] = part_advanced[:, cols] + added[0]
        adjoint[:, cols] = part_adjoint[:, cols] + added[1]
        for copy in results(chunk):
            copy.start()
        return carry

    lax.fori_loop(0, ELEMS // 128, close, 0, unroll=UNROLL_CLOSE)

    def finish(chunk, carry):
        for copy in results(chunk):
            copy.wait()
        return carry

    lax.fori_loop(0, ELEMS // 128, finish, 0)


def solution(mesh):
    n_dom = mesh.shape["dom"]
    matrices = nodal_matrices()
    forward_np = split_constant(matrices)
    backward_np = split_constant([matrix.T for matrix in matrices])
    expansion_np = face_expansion()
    in_hbm = pl.BlockSpec(memory_space=pltpu.HBM)
    in_vmem = pl.BlockSpec(memory_space=pltpu.VMEM)
    dma = pltpu.SemaphoreType.DMA
    field = jax.ShapeDtypeStruct((128, ELEMS), F32)

    def shards(
        state, cotangent, velocity, dispersion, retained, kappa, elem_block, face_source, send_face
    ):
        kept = functools.partial(pltpu.with_memory_space_constraint, memory_space=pltpu.HBM)
        forward_op = kept(jnp.asarray(forward_np))
        backward_op = kept(jnp.asarray(backward_np))
        expansion = kept(jnp.asarray(expansion_np))
        state, cotangent, velocity, retained = map(kept, (state, cotangent, velocity, retained))
        face_source, send_face, kappa = map(kept, (face_source, send_face, kappa))
        dispersion = kept(dispersion.reshape(1, ELEMS))
        elem_block = kept(elem_block.reshape(1, ELEMS))
        part_advanced, part_adjoint, arrived, sums, outer_rows = pl.pallas_call(
            functools.partial(exchange_kernel, n_dom),
            out_shape=(
                field,
                field,
                jax.ShapeDtypeStruct((ROUNDS, HALF, 128), F32),
                jax.ShapeDtypeStruct((N_SUB, 1, 128), F32),
                jax.ShapeDtypeStruct((FACES + 8, 128), F32),
            ),
            in_specs=[in_hbm] * 11,
            out_specs=(in_vmem,) * 5,
            scratch_shapes=[
                pltpu.VMEM((ELEMS // 128, 128, 128), F32),
                pltpu.VMEM((ELEMS // 128, 128, 128), F32),
                pltpu.VMEM((3, ELEMS), F32),
                pltpu.VMEM((1, ELEMS), F32),
                pltpu.VMEM((ELEMS // 128, 128, 128), F32),
                pltpu.VMEM((1, ELEMS), jnp.int32),
                pltpu.VMEM((512, 384), BF16),
                pltpu.VMEM((512, 384), BF16),
                pltpu.SMEM((16,), F32),
                pltpu.SMEM((FACES,), jnp.int32),
                pltpu.SMEM((ROUNDS * CAP,), jnp.int32),
                pltpu.VMEM((TABLE, 128), F32),
                pltpu.VMEM((ROUNDS, HALF, 128), F32),
                pltpu.VMEM((N_SUB, 1, 128), F32),
                pltpu.VMEM((1, 128), F32),
                pltpu.VMEM((16, 128), F32),
                dma((7,)),
                dma((3, ELEMS // 128)),
                dma((ROUNDS + 6,)),
                dma((ROUNDS,)),
                dma((ROUNDS,)),
                dma((N_SUB,)),
                dma((N_SUB,)),
                dma((N_SUB,)),
                dma((N_SUB,)),
            ],
            compiler_params=pltpu.CompilerParams(
                collective_id=0, has_side_effects=True, vmem_limit_bytes=40 << 20
            ),
            name="exchange",
        )(
            state,
            cotangent,
            velocity,
            dispersion,
            retained,
            kappa,
            elem_block,
            face_source,
            send_face,
            forward_op,
            backward_op,
        )
        advanced, adjoint, grad, _ = pl.pallas_call(
            merge_kernel,
            out_shape=(
                field,
                field,
                jax.ShapeDtypeStruct((1, 16), F32),
                jax.ShapeDtypeStruct((FACES + 8, 128), F32),
            ),
            in_specs=[in_vmem] * 5 + [in_hbm] * 3,
            out_specs=(in_hbm, in_hbm, in_vmem, in_vmem),
            input_output_aliases={4: 3},
            scratch_shapes=[
                pltpu.VMEM((128, ELEMS), F32),
                pltpu.VMEM((128, ELEMS), F32),
                pltpu.VMEM((3, ELEMS), F32),
                pltpu.VMEM((128, 384), BF16),
                pltpu.SMEM((ROUNDS * CAP,), jnp.int32),
                pltpu.VMEM((ROUNDS * CAP, 128), F32),
                dma((2,)),
                dma((ROUNDS,)),
                dma((2, ELEMS // 128)),
            ],
            compiler_params=pltpu.CompilerParams(vmem_limit_bytes=40 << 20),
            name="merge",
        )(part_advanced, part_adjoint, arrived, sums, outer_rows, velocity, send_face, expansion)
        return advanced, adjoint, grad.reshape(16)

    wide = P(None, ("dom", "sub"))
    flat = P(("dom", "sub"))
    return jax.shard_map(
        shards,
        mesh=mesh,
        in_specs=(wide, wide, wide, flat, wide, flat, flat, wide, wide),
        out_specs=(wide, wide, flat),
        check_vma=False,
    )
```

```python
import functools

import jax
import jax.numpy as jnp
import numpy as np
from jax import lax
from jax.experimental import pallas as pl
from jax.experimental.pallas import tpu as pltpu
from jax.sharding import PartitionSpec as P

REACH = 3
ROUNDS = 2 * REACH
STEP = 0.02
SECOND_SPECIES = 0.35
ELEMS = 1024
FACES = 6 * ELEMS
CAP = 384
HALF = CAP // 2
QUARTER = CAP // 4
TABLE = FACES + ROUNDS * CAP + 8
N_SUB = 8
BLOCKS = 128
UNROLL_BUILD = 1
UNROLL_CLOSE = 8
MESH = pl.DeviceIdType.MESH
F32 = jnp.float32
BF16 = jnp.bfloat16


def nodal_matrices():
    inner_point = 1.0 / np.sqrt(5.0)
    points = np.array([-1.0, -inner_point, inner_point, 1.0])
    bary_weight = np.array(
        [1.0 / np.prod([points[j] - points[m] for m in range(4) if m != j]) for j in range(4)]
    )
    derivative = np.zeros((4, 4))
    for i in range(4):
        for j in range(4):
            if i != j:
                derivative[i, j] = bary_weight[j] / bary_weight[i] / (points[i] - points[j])
        derivative[i, i] = -np.sum(derivative[i])
    identity = np.eye(4)
    along_i = np.kron(identity, np.kron(identity, derivative))
    along_j = np.kron(identity, np.kron(derivative, identity))
    along_k = np.kron(derivative, np.eye(16))
    second = along_i @ along_i + along_j @ along_j + along_k @ along_k
    return [np.kron(np.eye(2), matrix) for matrix in (along_i, along_j, along_k, second)]


def split_constant(matrices):
    stacked = np.concatenate(matrices, axis=0).astype(np.float32)
    high = stacked.astype(BF16)
    low = (stacked - high.astype(np.float32)).astype(BF16)
    return np.concatenate([high, high, low], axis=1)


def face_rows(face):
    rows = []
    for species in range(2):
        for slow in range(4):
            for fast in range(4):
                direction, last = face // 2, 3 * (face % 2)
                if direction == 0:
                    node = last + 4 * fast + 16 * slow
                elif direction == 1:
                    node = fast + 4 * last + 16 * slow
                else:
                    node = fast + 4 * slow + 16 * last
                rows.append(species * 64 + node)
    return rows


def face_expansion():
    expand = np.zeros((128, 192), np.float32)
    for face in range(6):
        for place, row in enumerate(face_rows(face)):
            expand[row, face * 32 + place] = 1.0
    return np.concatenate([expand, expand], axis=1).astype(BF16)


def split2(x):
    high = x.astype(BF16)
    return high, (x - high.astype(F32)).astype(BF16)


def split3(x):
    high, rest = x.astype(BF16), None
    rest = x - high.astype(F32)
    middle = rest.astype(BF16)
    return high, middle, (rest - middle.astype(F32)).astype(BF16)


def iota(shape, axis):
    return lax.broadcasted_iota(jnp.int32, shape, axis)


def trace_of(ref, face, chunk):
    direction, upper = face // 2, face % 2
    if direction == 0:
        return ref[chunk, pl.ds(3 * upper, 32, stride=4), :]
    if direction == 2:
        start = 48 * upper
        return jnp.concatenate(
            [ref[chunk, pl.ds(start, 16), :], ref[chunk, pl.ds(64 + start, 16), :]], axis=0
        )
    low_half = iota((8, 128), 0) < 4
    pieces = []
    for n in range(0, 8, 2):
        if upper == 0:
            first = ref[chunk, pl.ds(16 * n, 8), :]
            second = ref[chunk, pl.ds(16 * (n + 1) - 4, 8), :]
        else:
            first = ref[chunk, pl.ds(16 * n + 12, 8), :]
            second = ref[chunk, pl.ds(16 * (n + 1) + 8, 8), :]
        pieces.append(jnp.where(low_half, first, second))
    return jnp.concatenate(pieces, axis=0)


def face_weight(velocity, face):
    normal = velocity[face // 2 : face // 2 + 1]
    return 6.0 * jnp.minimum(normal if face % 2 else -normal, 0.0)


def expand_faces(pair_rows, velocity, expansion):
    outer_parts, back_parts = [], []
    for pair in range(3):
        columns = jnp.transpose(pair_rows(pair))
        for side in range(2):
            weight = face_weight(velocity, 2 * pair + side) * (-STEP)
            outer_parts.append(columns[64 * side : 64 * side + 32] * weight)
            back_parts.append(columns[64 * side + 32 : 64 * side + 64] * STEP)
    terms = jnp.concatenate(
        [jnp.concatenate(outer_parts, axis=0), jnp.concatenate(back_parts, axis=0)], axis=1
    )
    high, low = split2(terms)
    added = jnp.dot(
        expansion, jnp.concatenate([high, low], axis=0), preferred_element_type=F32
    )
    return added[:, :128], added[:, 128:]


def exchange_kernel(
    n_dom,
    state_hbm,
    cotangent_hbm,
    velocity_hbm,
    dispersion_hbm,
    retained_hbm,
    kappa_hbm,
    block_hbm,
    source_hbm,
    send_hbm,
    forward_hbm,
    backward_hbm,
    expansion_hbm,
    advanced,
    adjoint,
    arrived_out,
    sums_out,
    outer_rows,
    velocity,
    send_rows,
    expansion,
    state,
    cotangent,
    dispersion,
    retained,
    block,
    forward_op,
    backward_op,
    kappa_ref,
    source_index,
    send_index,
    table,
    outgoing,
    kappa_rows,
    sums_row,
    sums_acc,
    in_sem,
    field_sem,
    index_sem,
    send_sem,
    recv_sem,
    kappa_send,
    kappa_recv,
    sums_send,
    sums_recv,
):
    dom = lax.axis_index("dom")
    sub = lax.axis_index("sub")
    loads = {}
    for number, (name, src, dst) in enumerate(
        [
            ("velocity", velocity_hbm, velocity),
            ("kappa", kappa_hbm, kappa_ref),
            ("block", block_hbm, block),
            ("dispersion", dispersion_hbm, dispersion),
            ("forward", forward_hbm, forward_op),
            ("backward", backward_hbm, backward_op),
            ("rows", send_hbm, send_rows),
            ("expansion", expansion_hbm, expansion),
        ]
    ):
        loads[name] = pltpu.make_async_copy(src, dst, in_sem.at[number])
    send_loads = [
        pltpu.make_async_copy(
            send_hbm.at[number], send_index.at[pl.ds(number * CAP, CAP)], index_sem.at[number]
        )
        for number in range(ROUNDS)
    ]
    source_loads = [
        pltpu.make_async_copy(
            source_hbm.at[face],
            source_index.at[pl.ds(face * ELEMS, ELEMS)],
            index_sem.at[ROUNDS + face],
        )
        for face in range(6)
    ]

    def field_load(number, chunk):
        src, dst = ((state_hbm, state), (cotangent_hbm, cotangent), (retained_hbm, retained))[number]
        start = chunk * 128 if isinstance(chunk, int) else pl.multiple_of(chunk * 128, 128)
        return pltpu.make_async_copy(
            src.at[:, pl.ds(start, 128)], dst.at[chunk], field_sem.at[number, chunk]
        )

    loads["velocity"].start()
    for number in range(2):
        field_load(number, 0).start()

    def dom_partner(offset):
        return dom + offset

    def has_partner(offset):
        return dom >= -offset if offset < 0 else dom < n_dom - offset

    def sub_partner(turn):
        return lax.rem(sub + turn, N_SUB)

    offsets = [n - REACH if n < REACH else n - REACH + 1 for n in range(ROUNDS)]
    barrier = pltpu.get_barrier_semaphore()
    partner_count = N_SUB - 1
    for offset in offsets:
        partner_count = partner_count + has_partner(offset).astype(jnp.int32)

        @pl.when(has_partner(offset))
        def _(offset=offset):
            pl.semaphore_signal(
                barrier, inc=1, device_id={"dom": dom_partner(offset)}, device_id_type=MESH
            )

    for turn in range(1, N_SUB):
        pl.semaphore_signal(
            barrier, inc=1, device_id={"sub": sub_partner(turn)}, device_id_type=MESH
        )

    for chunk in range(1, ELEMS // 128):
        for number in range(2):
            field_load(number, chunk).start()
    for load in send_loads:
        load.start()
    loads["kappa"].start()

    zero_tile = jnp.zeros((8, 128), F32)

    def clear(step, carry):
        table[pl.ds(pl.multiple_of(FACES + step * 8, 8), 8), :] = zero_tile
        return carry

    lax.fori_loop(0, (TABLE - FACES) // 8, clear, 0, unroll=17)

    loads["velocity"].wait()
    def build(chunk, carry):
        field_load(0, chunk).wait()
        field_load(1, chunk).wait()
        start = pl.multiple_of(chunk * 128, 128)
        cols = pl.ds(start, 128)
        speeds = velocity[:, cols]
        for face in range(6):
            both = [
                trace_of(state, face, chunk),
                trace_of(cotangent, face, chunk) * (-face_weight(speeds, face)),
            ]
            table[pl.ds(pl.multiple_of(face * ELEMS + start, 128), 128), :] = jnp.transpose(
                jnp.concatenate(both + both, axis=0)
            )
        return carry

    lax.fori_loop(0, ELEMS // 128, build, 0, unroll=UNROLL_BUILD)
    low_row = iota((1, 128), 1) < 64

    for load in send_loads:
        load.wait()

    group = 32
    lane_row = iota((1, 128), 1)
    own_row = jnp.zeros((1, 128), F32)
    loads["kappa"].wait()
    for place in range(16):
        own_row = jnp.where(lane_row == sub * 16 + place, kappa_ref[place], own_row)
    kappa_rows[0] = own_row

    kappa_copies = [
        pltpu.make_async_remote_copy(
            src_ref=kappa_rows.at[0],
            dst_ref=kappa_rows.at[turn],
            send_sem=kappa_send.at[turn],
            recv_sem=kappa_recv.at[turn],
            device_id={"sub": sub_partner(turn)},
            device_id_type=MESH,
        )
        for turn in range(1, N_SUB)
    ]

    round_copies = []
    round_order = [(r, half) for r in ((0, 5), (1, 4), (2, 3)) for half in range(2)]
    round_order = [(number, half) for pair, half in round_order for number in pair]
    for turn, (number, half) in enumerate(round_order):

        def gather(step, carry, number=number):
            base = step * group
            values = []
            for place in range(group):
                first = send_index[number * CAP + base + place]
                second = send_index[number * CAP + HALF + base + place]
                values.append(
                    jnp.where(low_row, table[pl.ds(first, 1), :], table[pl.ds(second, 1), :])
                )
            for place in range(group):
                outgoing[number, pl.ds(base + place, 1), :] = values[place]
            return carry

        part = pl.ds(half * QUARTER, QUARTER)
        copy = pltpu.make_async_remote_copy(
            src_ref=outgoing.at[number, part],
            dst_ref=arrived_out.at[ROUNDS - 1 - number, part],
            send_sem=send_sem.at[number, half],
            recv_sem=recv_sem.at[ROUNDS - 1 - number, half],
            device_id={"dom": dom_partner(offsets[number])},
            device_id_type=MESH,
        )

        steps = QUARTER // group
        lax.fori_loop(half * steps, (half + 1) * steps, gather, 0)
        if turn == 0:
            pl.semaphore_wait(barrier, partner_count)
        pl.when(has_partner(offsets[number]))(copy.start)

        round_copies.append(copy)
        if turn == 3:
            for copy in kappa_copies:
                copy.start()
            loads["block"].start()
            for chunk in range(ELEMS // 128):
                field_load(2, chunk).start()
        if turn == 7:
            for load in source_loads:
                load.start()
            for name in ("dispersion", "forward", "backward", "rows", "expansion"):
                loads[name].start()

    width = 256
    sublane = iota((8, width), 0)

    def two_chunks(ref, chunk):
        return jnp.concatenate([ref[2 * chunk], ref[2 * chunk + 1]], axis=1)

    def free_sites(chunk):
        gain = jnp.where(iota((128, width), 0) < 64, 1.0, SECOND_SPECIES)
        return gain * (1.0 - two_chunks(retained, chunk))

    def block_hits(cols):
        return (iota((BLOCKS, width), 0) == block[:, cols]).astype(F32).astype(BF16)

    loads["block"].wait()
    for chunk in range(ELEMS // 128):
        field_load(2, chunk).wait()
    sums_acc[...] = jnp.zeros_like(sums_acc)

    def block_sums(chunk, carry):
        cols = pl.ds(pl.multiple_of(chunk * width, width), width)
        product = free_sites(chunk) * two_chunks(cotangent, chunk) * two_chunks(state, chunk)
        terms = jnp.sum(product, axis=0, keepdims=True)
        term_parts = jnp.concatenate(
            list(split3(terms)) + [jnp.zeros((13, width), BF16)], axis=0
        )
        sums_acc[...] += lax.dot_general(
            term_parts, block_hits(cols), (((1,), (1,)), ((), ())), preferred_element_type=F32
        )
        return carry

    lax.fori_loop(0, ELEMS // width, block_sums, 0)
    sums_row[...] = (sums_acc[0:1] + sums_acc[1:2]) + sums_acc[2:3]

    sums_out[0] = sums_row[...]
    sums_copies = [
        pltpu.make_async_remote_copy(
            src_ref=sums_row,
            dst_ref=sums_out.at[turn],
            send_sem=sums_send.at[turn],
            recv_sem=sums_recv.at[turn],
            device_id={"sub": sub_partner(turn)},
            device_id_type=MESH,
        )
        for turn in range(1, N_SUB)
    ]
    for copy in sums_copies:
        copy.start()

    for load in source_loads:
        load.wait()

    def pick(step, carry):
        base = step * (2 * group)
        values = [
            table[pl.ds(source_index[base + place], 1), :] for place in range(2 * group)
        ]
        for place in range(2 * group):
            outer_rows[pl.ds(base + place, 1), :] = values[place]
        return carry

    lax.fori_loop(0, FACES // (2 * group), pick, 0)

    for copy in kappa_copies:
        copy.wait_recv()
    slab = kappa_rows[0]
    for turn in range(1, N_SUB):
        slab = slab + kappa_rows[turn]
    slab_parts = jnp.concatenate(
        list(split3(slab)) + [jnp.zeros((13, 128), BF16)], axis=0
    )
    for name in ("dispersion", "forward", "backward", "rows", "expansion"):
        loads[name].wait()

    def volume(chunk, carry):
        start = pl.multiple_of(chunk * width, width)
        cols = pl.ds(start, width)
        rates = jnp.dot(slab_parts, block_hits(cols), preferred_element_type=F32)
        elem_rate = (rates[0:1] + rates[1:2]) + rates[2:3]
        speeds = velocity[:, cols]
        spread = dispersion[:, cols] * STEP

        field = two_chunks(state, chunk)
        dual = two_chunks(cotangent, chunk)
        weights = [face_weight(speeds, face) for face in range(6)]
        along_i = jnp.where(
            sublane % 4 == 0, weights[0], jnp.where(sublane % 4 == 3, weights[1], 0.0)
        )
        by_j = [
            along_i + jnp.where(sublane < 4, weights[2], 0.0),
            along_i + jnp.where(sublane >= 4, weights[3], 0.0),
        ]
        tiles = [by_j[0] + weights[4], by_j[1] + weights[4]]
        tiles += [by_j[0], by_j[1], by_j[0], by_j[1]]
        tiles += [by_j[0] + weights[5], by_j[1] + weights[5]]
        face_part = jnp.concatenate(tiles + tiles, axis=0)
        free = free_sites(chunk)
        factor = 1.0 + STEP * (face_part - elem_rate * free)
        for values, operator, target in (
            (field, forward_op, advanced),
            (dual, backward_op, adjoint),
        ):
            high, low = split2(values)
            images = jnp.dot(
                operator[...],
                jnp.concatenate([high, low, high], axis=0),
                preferred_element_type=F32,
            )
            target[:, cols] = (
                factor * values
                - (STEP * speeds[0:1]) * images[0:128]
                - (STEP * speeds[1:2]) * images[128:256]
                - (STEP * speeds[2:3]) * images[256:384]
                + spread * images[384:512]
            )
        return carry

    lax.fori_loop(0, ELEMS // width, volume, 0)
    for copy in kappa_copies:
        copy.wait_send()
    for copy in sums_copies:
        copy.wait()
    for (number, _), copy in zip(round_order, round_copies):
        pl.when(has_partner(offsets[number]))(copy.wait_send)
        pl.when(has_partner(offsets[ROUNDS - 1 - number]))(copy.wait_recv)


def merge_kernel(
    part_advanced,
    part_adjoint,
    arrived,
    sums,
    outer_rows,
    velocity,
    send_rows,
    expansion,
    advanced_out,
    adjoint_out,
    grad_out,
    spread,
    advanced,
    adjoint,
    send_index,
    rows,
    index_sem,
    out_sem,
):
    del outer_rows
    sub = lax.axis_index("sub")
    index_loads = [
        pltpu.make_async_copy(
            send_rows.at[number], send_index.at[pl.ds(number * CAP, CAP)], index_sem.at[number]
        )
        for number in range(ROUNDS)
    ]
    for load in index_loads:
        load.start()
    low_lanes = iota((HALF, 128), 1) < 64
    for number in range(ROUNDS):
        values = arrived[number]
        turned = pltpu.roll(values, 64, 1)
        rows[pl.ds(number * CAP, HALF), :] = jnp.where(low_lanes, values, turned)
        rows[pl.ds(number * CAP + HALF, HALF), :] = jnp.where(low_lanes, turned, values)
    for load in index_loads:
        load.wait()
    group = 384

    def scatter(step, carry):
        base = step * group
        values = [rows[pl.ds(base + place, 1), :] for place in range(group)]
        for place in range(group):
            spread[pl.ds(send_index[base + place], 1), :] = values[place]
        return carry

    lax.fori_loop(0, ROUNDS * CAP // group, scatter, 0)
    total = jnp.zeros((1, 128), F32)
    for turn in range(N_SUB):
        total = total + sums[turn]
    total = pltpu.roll(total, 128 - sub * 16, 1)
    grad_out[...] = -STEP * total[:, :16]
    low_part = iota((128, 128), 1) < 64

    def results(chunk):
        cols = pl.ds(pl.multiple_of(chunk * 128, 128), 128)
        return [
            pltpu.make_async_copy(
                advanced.at[:, cols], advanced_out.at[:, cols], out_sem.at[0, chunk]
            ),
            pltpu.make_async_copy(
                adjoint.at[:, cols], adjoint_out.at[:, cols], out_sem.at[1, chunk]
            ),
        ]

    def close(chunk, carry):
        start = pl.multiple_of(chunk * 128, 128)
        cols = pl.ds(start, 128)

        def pair_rows(pair):
            first = spread[pl.ds(pl.multiple_of(2 * pair * ELEMS + start, 128), 128), :]
            second = spread[pl.ds(pl.multiple_of((2 * pair + 1) * ELEMS + start, 128), 128), :]
            return jnp.where(low_part, first, second)

        added = expand_faces(pair_rows, velocity[:, cols], expansion[...])
        advanced[:, cols] = part_advanced[:, cols] + added[0]
        adjoint[:, cols] = part_adjoint[:, cols] + added[1]
        for copy in results(chunk):
            copy.start()
        return carry

    lax.fori_loop(0, ELEMS // 128, close, 0, unroll=UNROLL_CLOSE)

    def finish(chunk, carry):
        for copy in results(chunk):
            copy.wait()
        return carry

    lax.fori_loop(0, ELEMS // 128, finish, 0)


def solution(mesh):
    n_dom = mesh.shape["dom"]
    matrices = nodal_matrices()
    forward_np = split_constant(matrices)
    backward_np = split_constant([matrix.T for matrix in matrices])
    expansion_np = face_expansion()
    in_hbm = pl.BlockSpec(memory_space=pltpu.HBM)
    in_vmem = pl.BlockSpec(memory_space=pltpu.VMEM)
    dma = pltpu.SemaphoreType.DMA
    field = jax.ShapeDtypeStruct((128, ELEMS), F32)

    def shards(
        state, cotangent, velocity, dispersion, retained, kappa, elem_block, face_source, send_face
    ):
        kept = functools.partial(pltpu.with_memory_space_constraint, memory_space=pltpu.HBM)
        forward_op = kept(jnp.asarray(forward_np))
        backward_op = kept(jnp.asarray(backward_np))
        expansion = kept(jnp.asarray(expansion_np))
        state, cotangent, velocity, retained = map(kept, (state, cotangent, velocity, retained))
        face_source, send_face, kappa = map(kept, (face_source, send_face, kappa))
        dispersion = kept(dispersion.reshape(1, ELEMS))
        elem_block = kept(elem_block.reshape(1, ELEMS))
        handed_on = pl.pallas_call(
            functools.partial(exchange_kernel, n_dom),
            out_shape=(
                field,
                field,
                jax.ShapeDtypeStruct((ROUNDS, HALF, 128), F32),
                jax.ShapeDtypeStruct((N_SUB, 1, 128), F32),
                jax.ShapeDtypeStruct((FACES + 8, 128), F32),
                jax.ShapeDtypeStruct((3, ELEMS), F32),
                jax.ShapeDtypeStruct((ROUNDS, CAP), jnp.int32),
                jax.ShapeDtypeStruct((128, 384), BF16),
            ),
            in_specs=[in_hbm] * 12,
            out_specs=(in_vmem,) * 8,
            scratch_shapes=[
                pltpu.VMEM((ELEMS // 128, 128, 128), F32),
                pltpu.VMEM((ELEMS // 128, 128, 128), F32),
                pltpu.VMEM((1, ELEMS), F32),
                pltpu.VMEM((ELEMS // 128, 128, 128), F32),
                pltpu.VMEM((1, ELEMS), jnp.int32),
                pltpu.VMEM((512, 384), BF16),
                pltpu.VMEM((512, 384), BF16),
                pltpu.SMEM((16,), F32),
                pltpu.SMEM((FACES,), jnp.int32),
                pltpu.SMEM((ROUNDS * CAP,), jnp.int32),
                pltpu.VMEM((TABLE, 128), F32),
                pltpu.VMEM((ROUNDS, HALF, 128), F32),
                pltpu.VMEM((N_SUB, 1, 128), F32),
                pltpu.VMEM((1, 128), F32),
                pltpu.VMEM((16, 128), F32),
                dma((9,)),
                dma((3, ELEMS // 128)),
                dma((ROUNDS + 6,)),
                dma((ROUNDS, 2)),
                dma((ROUNDS, 2)),
                dma((N_SUB,)),
                dma((N_SUB,)),
                dma((N_SUB,)),
                dma((N_SUB,)),
            ],
            compiler_params=pltpu.CompilerParams(
                collective_id=0, has_side_effects=True, vmem_limit_bytes=40 << 20
            ),
            name="exchange",
        )(
            state,
            cotangent,
            velocity,
            dispersion,
            retained,
            kappa,
            elem_block,
            face_source,
            send_face,
            forward_op,
            backward_op,
            expansion,
        )
        advanced, adjoint, grad, _ = pl.pallas_call(
            merge_kernel,
            out_shape=(
                field,
                field,
                jax.ShapeDtypeStruct((1, 16), F32),
                jax.ShapeDtypeStruct((FACES + 8, 128), F32),
            ),
            in_specs=[in_vmem] * 8,
            out_specs=(in_hbm, in_hbm, in_vmem, in_vmem),
            input_output_aliases={4: 3},
            scratch_shapes=[
                pltpu.VMEM((128, ELEMS), F32),
                pltpu.VMEM((128, ELEMS), F32),
                pltpu.SMEM((ROUNDS * CAP,), jnp.int32),
                pltpu.VMEM((ROUNDS * CAP, 128), F32),
                dma((ROUNDS,)),
                dma((2, ELEMS // 128)),
            ],
            compiler_params=pltpu.CompilerParams(vmem_limit_bytes=40 << 20),
            name="merge",
        )(*handed_on)
        return advanced, adjoint, grad.reshape(16)

    wide = P(None, ("dom", "sub"))
    flat = P(("dom", "sub"))
    return jax.shard_map(
        shards,
        mesh=mesh,
        in_specs=(wide, wide, wide, flat, wide, flat, flat, wide, wide),
        out_specs=(wide, wide, flat),
        check_vma=False,
    )
```

```python
import functools

import jax
import jax.numpy as jnp
import numpy as np
from jax import lax
from jax.experimental import pallas as pl
from jax.experimental.pallas import tpu as pltpu
from jax.sharding import PartitionSpec as P

REACH = 3
ROUNDS = 2 * REACH
STEP = 0.02
SECOND_SPECIES = 0.35
ELEMS = 1024
FACES = 6 * ELEMS
CAP = 384
HALF = CAP // 2
QUARTER = CAP // 4
TABLE = FACES + ROUNDS * CAP + 8
N_SUB = 8
BLOCKS = 128
UNROLL_CLOSE = 8
MESH = pl.DeviceIdType.MESH
F32 = jnp.float32
BF16 = jnp.bfloat16


def nodal_matrices():
    inner_point = 1.0 / np.sqrt(5.0)
    points = np.array([-1.0, -inner_point, inner_point, 1.0])
    bary_weight = np.array(
        [1.0 / np.prod([points[j] - points[m] for m in range(4) if m != j]) for j in range(4)]
    )
    derivative = np.zeros((4, 4))
    for i in range(4):
        for j in range(4):
            if i != j:
                derivative[i, j] = bary_weight[j] / bary_weight[i] / (points[i] - points[j])
        derivative[i, i] = -np.sum(derivative[i])
    identity = np.eye(4)
    along_i = np.kron(identity, np.kron(identity, derivative))
    along_j = np.kron(identity, np.kron(derivative, identity))
    along_k = np.kron(derivative, np.eye(16))
    second = along_i @ along_i + along_j @ along_j + along_k @ along_k
    return [np.kron(np.eye(2), matrix) for matrix in (along_i, along_j, along_k, second)]


def split_constant(matrices):
    stacked = np.concatenate(matrices, axis=0).astype(np.float32)
    high = stacked.astype(BF16)
    low = (stacked - high.astype(np.float32)).astype(BF16)
    return np.concatenate([high, high, low], axis=1)


def face_rows(face):
    rows = []
    for species in range(2):
        for slow in range(4):
            for fast in range(4):
                direction, last = face // 2, 3 * (face % 2)
                if direction == 0:
                    node = last + 4 * fast + 16 * slow
                elif direction == 1:
                    node = fast + 4 * last + 16 * slow
                else:
                    node = fast + 4 * slow + 16 * last
                rows.append(species * 64 + node)
    return rows


def face_expansion():
    expand = np.zeros((128, 192), np.float32)
    for face in range(6):
        for place, row in enumerate(face_rows(face)):
            expand[row, face * 32 + place] = 1.0
    return np.concatenate([expand, expand], axis=1).astype(BF16)


def split2(x):
    high = x.astype(BF16)
    return high, (x - high.astype(F32)).astype(BF16)


def split3(x):
    high, rest = x.astype(BF16), None
    rest = x - high.astype(F32)
    middle = rest.astype(BF16)
    return high, middle, (rest - middle.astype(F32)).astype(BF16)


def iota(shape, axis):
    return lax.broadcasted_iota(jnp.int32, shape, axis)


def trace_of(ref, face, chunk):
    direction, upper = face // 2, face % 2
    if direction == 0:
        return ref[chunk, pl.ds(3 * upper, 32, stride=4), :]
    if direction == 2:
        start = 48 * upper
        return jnp.concatenate(
            [ref[chunk, pl.ds(start, 16), :], ref[chunk, pl.ds(64 + start, 16), :]], axis=0
        )
    low_half = iota((8, 128), 0) < 4
    pieces = []
    for n in range(0, 8, 2):
        if upper == 0:
            first = ref[chunk, pl.ds(16 * n, 8), :]
            second = ref[chunk, pl.ds(16 * (n + 1) - 4, 8), :]
        else:
            first = ref[chunk, pl.ds(16 * n + 12, 8), :]
            second = ref[chunk, pl.ds(16 * (n + 1) + 8, 8), :]
        pieces.append(jnp.where(low_half, first, second))
    return jnp.concatenate(pieces, axis=0)


def face_weight(velocity, face):
    normal = velocity[face // 2 : face // 2 + 1]
    return 6.0 * jnp.minimum(normal if face % 2 else -normal, 0.0)


def expand_faces(pair_rows, velocity, expansion):
    outer_parts, back_parts = [], []
    for pair in range(3):
        columns = jnp.transpose(pair_rows(pair))
        for side in range(2):
            weight = face_weight(velocity, 2 * pair + side) * (-STEP)
            outer_parts.append(columns[64 * side : 64 * side + 32] * weight)
            back_parts.append(columns[64 * side + 32 : 64 * side + 64] * STEP)
    terms = jnp.concatenate(
        [jnp.concatenate(outer_parts, axis=0), jnp.concatenate(back_parts, axis=0)], axis=1
    )
    high, low = split2(terms)
    added = jnp.dot(
        expansion, jnp.concatenate([high, low], axis=0), preferred_element_type=F32
    )
    return added[:, :128], added[:, 128:]


def exchange_kernel(
    n_dom,
    state_hbm,
    cotangent_hbm,
    velocity_hbm,
    dispersion_hbm,
    retained_hbm,
    kappa_hbm,
    block_hbm,
    source_hbm,
    send_hbm,
    forward_hbm,
    backward_hbm,
    expansion_hbm,
    advanced,
    adjoint,
    arrived_out,
    sums_out,
    outer_rows,
    velocity,
    send_rows,
    expansion,
    state,
    cotangent,
    dispersion,
    retained,
    block,
    forward_op,
    backward_op,
    kappa_ref,
    source_index,
    send_index,
    table,
    outgoing,
    kappa_rows,
    sums_row,
    sums_acc,
    in_sem,
    field_sem,
    index_sem,
    send_sem,
    recv_sem,
    kappa_send,
    kappa_recv,
    sums_send,
    sums_recv,
):
    dom = lax.axis_index("dom")
    sub = lax.axis_index("sub")
    loads = {}
    for number, (name, src, dst) in enumerate(
        [
            ("velocity", velocity_hbm, velocity),
            ("kappa", kappa_hbm, kappa_ref),
            ("block", block_hbm, block),
            ("dispersion", dispersion_hbm, dispersion),
            ("forward", forward_hbm, forward_op),
            ("backward", backward_hbm, backward_op),
            ("rows", send_hbm, send_rows),
            ("expansion", expansion_hbm, expansion),
        ]
    ):
        loads[name] = pltpu.make_async_copy(src, dst, in_sem.at[number])
    send_loads = [
        pltpu.make_async_copy(
            send_hbm.at[number], send_index.at[pl.ds(number * CAP, CAP)], index_sem.at[number]
        )
        for number in range(ROUNDS)
    ]
    source_loads = [
        pltpu.make_async_copy(
            source_hbm.at[face],
            source_index.at[pl.ds(face * ELEMS, ELEMS)],
            index_sem.at[ROUNDS + face],
        )
        for face in range(6)
    ]

    def field_load(number, chunk):
        src, dst = ((state_hbm, state), (cotangent_hbm, cotangent), (retained_hbm, retained))[number]
        start = chunk * 128 if isinstance(chunk, int) else pl.multiple_of(chunk * 128, 128)
        return pltpu.make_async_copy(
            src.at[:, pl.ds(start, 128)], dst.at[chunk], field_sem.at[number, chunk]
        )

    loads["velocity"].start()
    for number in range(2):
        field_load(number, 0).start()

    def dom_partner(offset):
        return dom + offset

    def has_partner(offset):
        return dom >= -offset if offset < 0 else dom < n_dom - offset

    def sub_partner(turn):
        return lax.rem(sub + turn, N_SUB)

    offsets = [n - REACH if n < REACH else n - REACH + 1 for n in range(ROUNDS)]
    barrier = pltpu.get_barrier_semaphore()
    partner_count = N_SUB - 1
    for offset in offsets:
        partner_count = partner_count + has_partner(offset).astype(jnp.int32)

        @pl.when(has_partner(offset))
        def _(offset=offset):
            pl.semaphore_signal(
                barrier, inc=1, device_id={"dom": dom_partner(offset)}, device_id_type=MESH
            )

    for turn in range(1, N_SUB):
        pl.semaphore_signal(
            barrier, inc=1, device_id={"sub": sub_partner(turn)}, device_id_type=MESH
        )

    for chunk in range(1, ELEMS // 128):
        for number in range(2):
            field_load(number, chunk).start()
    for load in send_loads:
        load.start()
    loads["kappa"].start()

    zero_tile = jnp.zeros((8, 128), F32)

    def clear(step, carry):
        table[pl.ds(pl.multiple_of(FACES + step * 8, 8), 8), :] = zero_tile
        return carry

    lax.fori_loop(0, (TABLE - FACES) // 8, clear, 0, unroll=17)

    loads["velocity"].wait()
    def build(chunk, carry):
        field_load(0, chunk).wait()
        field_load(1, chunk).wait()
        start = pl.multiple_of(chunk * 128, 128)
        cols = pl.ds(start, 128)
        speeds = velocity[:, cols]
        for face in range(6):
            both = [
                trace_of(state, face, chunk),
                trace_of(cotangent, face, chunk) * (-face_weight(speeds, face)),
            ]
            table[pl.ds(pl.multiple_of(face * ELEMS + start, 128), 128), :] = jnp.transpose(
                jnp.concatenate(both + both, axis=0)
            )
        return carry

    lax.fori_loop(0, ELEMS // 128, build, 0)
    low_row = iota((1, 128), 1) < 64

    for load in send_loads:
        load.wait()

    group = 32
    lane_row = iota((1, 128), 1)
    own_row = jnp.zeros((1, 128), F32)
    loads["kappa"].wait()
    for place in range(16):
        own_row = jnp.where(lane_row == sub * 16 + place, kappa_ref[place], own_row)
    kappa_rows[0] = own_row

    kappa_copies = [
        pltpu.make_async_remote_copy(
            src_ref=kappa_rows.at[0],
            dst_ref=kappa_rows.at[turn],
            send_sem=kappa_send.at[turn],
            recv_sem=kappa_recv.at[turn],
            device_id={"sub": sub_partner(turn)},
            device_id_type=MESH,
        )
        for turn in range(1, N_SUB)
    ]

    round_copies = []
    round_order = [(r, half) for r in ((0, 5), (2, 3), (1, 4)) for half in range(2)]
    round_order = [(number, half) for pair, half in round_order for number in pair]
    for turn, (number, half) in enumerate(round_order):

        def gather(step, carry, number=number):
            base = step * group
            values = []
            for place in range(group):
                first = send_index[number * CAP + base + place]
                second = send_index[number * CAP + HALF + base + place]
                values.append(
                    jnp.where(low_row, table[pl.ds(first, 1), :], table[pl.ds(second, 1), :])
                )
            for place in range(group):
                outgoing[number, pl.ds(base + place, 1), :] = values[place]
            return carry

        part = pl.ds(half * QUARTER, QUARTER)
        copy = pltpu.make_async_remote_copy(
            src_ref=outgoing.at[number, part],
            dst_ref=arrived_out.at[ROUNDS - 1 - number, part],
            send_sem=send_sem.at[number, half],
            recv_sem=recv_sem.at[ROUNDS - 1 - number, half],
            device_id={"dom": dom_partner(offsets[number])},
            device_id_type=MESH,
        )

        steps = QUARTER // group
        lax.fori_loop(half * steps, (half + 1) * steps, gather, 0)
        if turn == 0:
            pl.semaphore_wait(barrier, partner_count)
        pl.when(has_partner(offsets[number]))(copy.start)

        round_copies.append(copy)
        if turn == 3:
            for copy in kappa_copies:
                copy.start()
            loads["block"].start()
            for chunk in range(ELEMS // 128):
                field_load(2, chunk).start()
        if turn == 7:
            for load in source_loads:
                load.start()
            for name in ("dispersion", "forward", "backward", "rows", "expansion"):
                loads[name].start()

    width = 256
    sublane = iota((8, width), 0)

    def two_chunks(ref, chunk):
        return jnp.concatenate([ref[2 * chunk], ref[2 * chunk + 1]], axis=1)

    def free_sites(chunk):
        gain = jnp.where(iota((128, width), 0) < 64, 1.0, SECOND_SPECIES)
        return gain * (1.0 - two_chunks(retained, chunk))

    def block_hits(cols):
        return (iota((BLOCKS, width), 0) == block[:, cols]).astype(F32).astype(BF16)

    loads["block"].wait()
    for chunk in range(ELEMS // 128):
        field_load(2, chunk).wait()
    sums_acc[...] = jnp.zeros_like(sums_acc)

    def block_sums(chunk, carry):
        cols = pl.ds(pl.multiple_of(chunk * width, width), width)
        product = free_sites(chunk) * two_chunks(cotangent, chunk) * two_chunks(state, chunk)
        terms = jnp.sum(product, axis=0, keepdims=True)
        term_parts = jnp.concatenate(
            list(split3(terms)) + [jnp.zeros((13, width), BF16)], axis=0
        )
        sums_acc[...] += lax.dot_general(
            term_parts, block_hits(cols), (((1,), (1,)), ((), ())), preferred_element_type=F32
        )
        return carry

    lax.fori_loop(0, ELEMS // width, block_sums, 0)
    sums_row[...] = (sums_acc[0:1] + sums_acc[1:2]) + sums_acc[2:3]

    sums_out[0] = sums_row[...]
    sums_copies = [
        pltpu.make_async_remote_copy(
            src_ref=sums_row,
            dst_ref=sums_out.at[turn],
            send_sem=sums_send.at[turn],
            recv_sem=sums_recv.at[turn],
            device_id={"sub": sub_partner(turn)},
            device_id_type=MESH,
        )
        for turn in range(1, N_SUB)
    ]
    for copy in sums_copies:
        copy.start()

    for copy in kappa_copies:
        copy.wait_recv()
    slab = kappa_rows[0]
    for turn in range(1, N_SUB):
        slab = slab + kappa_rows[turn]
    slab_parts = jnp.concatenate(
        list(split3(slab)) + [jnp.zeros((13, 128), BF16)], axis=0
    )
    for name in ("dispersion", "forward", "backward", "rows", "expansion"):
        loads[name].wait()

    def volume(chunk, carry):
        start = pl.multiple_of(chunk * width, width)
        cols = pl.ds(start, width)
        rates = jnp.dot(slab_parts, block_hits(cols), preferred_element_type=F32)
        elem_rate = (rates[0:1] + rates[1:2]) + rates[2:3]
        speeds = velocity[:, cols]
        spread = dispersion[:, cols] * STEP

        field = two_chunks(state, chunk)
        dual = two_chunks(cotangent, chunk)
        weights = [face_weight(speeds, face) for face in range(6)]
        along_i = jnp.where(
            sublane % 4 == 0, weights[0], jnp.where(sublane % 4 == 3, weights[1], 0.0)
        )
        by_j = [
            along_i + jnp.where(sublane < 4, weights[2], 0.0),
            along_i + jnp.where(sublane >= 4, weights[3], 0.0),
        ]
        tiles = [by_j[0] + weights[4], by_j[1] + weights[4]]
        tiles += [by_j[0], by_j[1], by_j[0], by_j[1]]
        tiles += [by_j[0] + weights[5], by_j[1] + weights[5]]
        face_part = jnp.concatenate(tiles + tiles, axis=0)
        free = free_sites(chunk)
        factor = 1.0 + STEP * (face_part - elem_rate * free)
        for values, operator, target in (
            (field, forward_op, advanced),
            (dual, backward_op, adjoint),
        ):
            high, low = split2(values)
            images = jnp.dot(
                operator[...],
                jnp.concatenate([high, low, high], axis=0),
                preferred_element_type=F32,
            )
            target[:, cols] = (
                factor * values
                - (STEP * speeds[0:1]) * images[0:128]
                - (STEP * speeds[1:2]) * images[128:256]
                - (STEP * speeds[2:3]) * images[256:384]
                + spread * images[384:512]
            )
        return carry

    lax.fori_loop(0, ELEMS // width, volume, 0)
    for load in source_loads:
        load.wait()

    def pick(step, carry):
        base = step * (2 * group)
        values = [
            table[pl.ds(source_index[base + place], 1), :] for place in range(2 * group)
        ]
        for place in range(2 * group):
            outer_rows[pl.ds(base + place, 1), :] = values[place]
        return carry

    lax.fori_loop(0, FACES // (2 * group), pick, 0)

    for copy in kappa_copies:
        copy.wait_send()
    for copy in sums_copies:
        copy.wait()
    for (number, _), copy in zip(round_order, round_copies):
        pl.when(has_partner(offsets[number]))(copy.wait_send)
        pl.when(has_partner(offsets[ROUNDS - 1 - number]))(copy.wait_recv)


def merge_kernel(
    part_advanced,
    part_adjoint,
    arrived,
    sums,
    outer_rows,
    velocity,
    send_rows,
    expansion,
    advanced_out,
    adjoint_out,
    grad_out,
    spread,
    advanced,
    adjoint,
    send_index,
    rows,
    index_sem,
    out_sem,
):
    del outer_rows
    sub = lax.axis_index("sub")
    index_loads = [
        pltpu.make_async_copy(
            send_rows.at[number], send_index.at[pl.ds(number * CAP, CAP)], index_sem.at[number]
        )
        for number in range(ROUNDS)
    ]
    for load in index_loads:
        load.start()
    low_lanes = iota((HALF, 128), 1) < 64
    for number in range(ROUNDS):
        values = arrived[number]
        turned = pltpu.roll(values, 64, 1)
        rows[pl.ds(number * CAP, HALF), :] = jnp.where(low_lanes, values, turned)
        rows[pl.ds(number * CAP + HALF, HALF), :] = jnp.where(low_lanes, turned, values)
    for load in index_loads:
        load.wait()
    group = 384
    for number in range(ROUNDS):

        def scatter(step, carry, number=number):
            base = number * CAP + step * group
            values = [rows[pl.ds(base + place, 1), :] for place in range(group)]
            for place in range(group):
                spread[pl.ds(send_index[base + place], 1), :] = values[place]
            return carry

        lax.fori_loop(0, CAP // group, scatter, 0)
    total = jnp.zeros((1, 128), F32)
    for turn in range(N_SUB):
        total = total + sums[turn]
    total = pltpu.roll(total, 128 - sub * 16, 1)
    grad_out[...] = -STEP * total[:, :16]
    low_part = iota((128, 128), 1) < 64

    def results(chunk):
        cols = pl.ds(pl.multiple_of(chunk * 128, 128), 128)
        return [
            pltpu.make_async_copy(
                advanced.at[:, cols], advanced_out.at[:, cols], out_sem.at[0, chunk]
            ),
            pltpu.make_async_copy(
                adjoint.at[:, cols], adjoint_out.at[:, cols], out_sem.at[1, chunk]
            ),
        ]

    def close(chunk, carry):
        start = pl.multiple_of(chunk * 128, 128)
        cols = pl.ds(start, 128)

        def pair_rows(pair):
            first = spread[pl.ds(pl.multiple_of(2 * pair * ELEMS + start, 128), 128), :]
            second = spread[pl.ds(pl.multiple_of((2 * pair + 1) * ELEMS + start, 128), 128), :]
            return jnp.where(low_part, first, second)

        added = expand_faces(pair_rows, velocity[:, cols], expansion[...])
        advanced[:, cols] = part_advanced[:, cols] + added[0]
        adjoint[:, cols] = part_adjoint[:, cols] + added[1]
        for copy in results(chunk):
            copy.start()
        return carry

    lax.fori_loop(0, ELEMS // 128, close, 0, unroll=UNROLL_CLOSE)

    def finish(chunk, carry):
        for copy in results(chunk):
            copy.wait()
        return carry

    lax.fori_loop(0, ELEMS // 128, finish, 0)


def solution(mesh):
    n_dom = mesh.shape["dom"]
    matrices = nodal_matrices()
    forward_np = split_constant(matrices)
    backward_np = split_constant([matrix.T for matrix in matrices])
    expansion_np = face_expansion()
    in_hbm = pl.BlockSpec(memory_space=pltpu.HBM)
    in_vmem = pl.BlockSpec(memory_space=pltpu.VMEM)
    dma = pltpu.SemaphoreType.DMA
    field = jax.ShapeDtypeStruct((128, ELEMS), F32)

    def shards(
        state, cotangent, velocity, dispersion, retained, kappa, elem_block, face_source, send_face
    ):
        kept = functools.partial(pltpu.with_memory_space_constraint, memory_space=pltpu.HBM)
        forward_op = kept(jnp.asarray(forward_np))
        backward_op = kept(jnp.asarray(backward_np))
        expansion = kept(jnp.asarray(expansion_np))
        state, cotangent, velocity, retained = map(kept, (state, cotangent, velocity, retained))
        face_source, send_face, kappa = map(kept, (face_source, send_face, kappa))
        dispersion = kept(dispersion.reshape(1, ELEMS))
        elem_block = kept(elem_block.reshape(1, ELEMS))
        handed_on = pl.pallas_call(
            functools.partial(exchange_kernel, n_dom),
            out_shape=(
                field,
                field,
                jax.ShapeDtypeStruct((ROUNDS, HALF, 128), F32),
                jax.ShapeDtypeStruct((N_SUB, 1, 128), F32),
                jax.ShapeDtypeStruct((FACES + 8, 128), F32),
                jax.ShapeDtypeStruct((3, ELEMS), F32),
                jax.ShapeDtypeStruct((ROUNDS, CAP), jnp.int32),
                jax.ShapeDtypeStruct((128, 384), BF16),
            ),
            in_specs=[in_hbm] * 12,
            out_specs=(in_vmem,) * 8,
            scratch_shapes=[
                pltpu.VMEM((ELEMS // 128, 128, 128), F32),
                pltpu.VMEM((ELEMS // 128, 128, 128), F32),
                pltpu.VMEM((1, ELEMS), F32),
                pltpu.VMEM((ELEMS // 128, 128, 128), F32),
                pltpu.VMEM((1, ELEMS), jnp.int32),
                pltpu.VMEM((512, 384), BF16),
                pltpu.VMEM((512, 384), BF16),
                pltpu.SMEM((16,), F32),
                pltpu.SMEM((FACES,), jnp.int32),
                pltpu.SMEM((ROUNDS * CAP,), jnp.int32),
                pltpu.VMEM((TABLE, 128), F32),
                pltpu.VMEM((ROUNDS, HALF, 128), F32),
                pltpu.VMEM((N_SUB, 1, 128), F32),
                pltpu.VMEM((1, 128), F32),
                pltpu.VMEM((16, 128), F32),
                dma((9,)),
                dma((3, ELEMS // 128)),
                dma((ROUNDS + 6,)),
                dma((ROUNDS, 2)),
                dma((ROUNDS, 2)),
                dma((N_SUB,)),
                dma((N_SUB,)),
                dma((N_SUB,)),
                dma((N_SUB,)),
            ],
            compiler_params=pltpu.CompilerParams(
                collective_id=0, has_side_effects=True, vmem_limit_bytes=40 << 20
            ),
            name="exchange",
        )(
            state,
            cotangent,
            velocity,
            dispersion,
            retained,
            kappa,
            elem_block,
            face_source,
            send_face,
            forward_op,
            backward_op,
            expansion,
        )
        advanced, adjoint, grad, _ = pl.pallas_call(
            merge_kernel,
            out_shape=(
                field,
                field,
                jax.ShapeDtypeStruct((1, 16), F32),
                jax.ShapeDtypeStruct((FACES + 8, 128), F32),
            ),
            in_specs=[in_vmem] * 8,
            out_specs=(in_hbm, in_hbm, in_vmem, in_vmem),
            input_output_aliases={4: 3},
            scratch_shapes=[
                pltpu.VMEM((128, ELEMS), F32),
                pltpu.VMEM((128, ELEMS), F32),
                pltpu.SMEM((ROUNDS * CAP,), jnp.int32),
                pltpu.VMEM((ROUNDS * CAP, 128), F32),
                dma((ROUNDS,)),
                dma((2, ELEMS // 128)),
            ],
            compiler_params=pltpu.CompilerParams(vmem_limit_bytes=40 << 20),
            name="merge",
        )(*handed_on)
        return advanced, adjoint, grad.reshape(16)

    wide = P(None, ("dom", "sub"))
    flat = P(("dom", "sub"))
    return jax.shard_map(
        shards,
        mesh=mesh,
        in_specs=(wide, wide, wide, flat, wide, flat, flat, wide, wide),
        out_specs=(wide, wide, flat),
        check_vma=False,
    )
```

```python
import functools

import jax
import jax.numpy as jnp
import numpy as np
from jax import lax
from jax.experimental import pallas as pl
from jax.experimental.pallas import tpu as pltpu
from jax.sharding import PartitionSpec as P

REACH = 3
ROUNDS = 2 * REACH
STEP = 0.02
SECOND_SPECIES = 0.35
ELEMS = 1024
FACES = 6 * ELEMS
CAP = 384
HALF = CAP // 2
QUARTER = CAP // 4
TABLE = FACES + ROUNDS * CAP + 8
N_SUB = 8
BLOCKS = 128
UNROLL_CLOSE = 8
MESH = pl.DeviceIdType.MESH
F32 = jnp.float32
BF16 = jnp.bfloat16


def nodal_matrices():
    inner_point = 1.0 / np.sqrt(5.0)
    points = np.array([-1.0, -inner_point, inner_point, 1.0])
    bary_weight = np.array(
        [1.0 / np.prod([points[j] - points[m] for m in range(4) if m != j]) for j in range(4)]
    )
    derivative = np.zeros((4, 4))
    for i in range(4):
        for j in range(4):
            if i != j:
                derivative[i, j] = bary_weight[j] / bary_weight[i] / (points[i] - points[j])
        derivative[i, i] = -np.sum(derivative[i])
    identity = np.eye(4)
    along_i = np.kron(identity, np.kron(identity, derivative))
    along_j = np.kron(identity, np.kron(derivative, identity))
    along_k = np.kron(derivative, np.eye(16))
    second = along_i @ along_i + along_j @ along_j + along_k @ along_k
    return [np.kron(np.eye(2), matrix) for matrix in (along_i, along_j, along_k, second)]


def split_constant(matrices):
    stacked = np.concatenate(matrices, axis=0).astype(np.float32)
    high = stacked.astype(BF16)
    low = (stacked - high.astype(np.float32)).astype(BF16)
    return np.concatenate([high, high, low], axis=1)


def face_rows(face):
    rows = []
    for species in range(2):
        for slow in range(4):
            for fast in range(4):
                direction, last = face // 2, 3 * (face % 2)
                if direction == 0:
                    node = last + 4 * fast + 16 * slow
                elif direction == 1:
                    node = fast + 4 * last + 16 * slow
                else:
                    node = fast + 4 * slow + 16 * last
                rows.append(species * 64 + node)
    return rows


def face_expansion():
    expand = np.zeros((128, 192), np.float32)
    for face in range(6):
        for place, row in enumerate(face_rows(face)):
            expand[row, face * 32 + place] = 1.0
    return np.concatenate([expand, expand], axis=1).astype(BF16)


def split2(x):
    high = x.astype(BF16)
    return high, (x - high.astype(F32)).astype(BF16)


def split3(x):
    high, rest = x.astype(BF16), None
    rest = x - high.astype(F32)
    middle = rest.astype(BF16)
    return high, middle, (rest - middle.astype(F32)).astype(BF16)


def iota(shape, axis):
    return lax.broadcasted_iota(jnp.int32, shape, axis)


def trace_of(ref, face, chunk):
    direction, upper = face // 2, face % 2
    if direction == 0:
        return ref[chunk, pl.ds(3 * upper, 32, stride=4), :]
    if direction == 2:
        start = 48 * upper
        return jnp.concatenate(
            [ref[chunk, pl.ds(start, 16), :], ref[chunk, pl.ds(64 + start, 16), :]], axis=0
        )
    low_half = iota((8, 128), 0) < 4
    pieces = []
    for n in range(0, 8, 2):
        if upper == 0:
            first = ref[chunk, pl.ds(16 * n, 8), :]
            second = ref[chunk, pl.ds(16 * (n + 1) - 4, 8), :]
        else:
            first = ref[chunk, pl.ds(16 * n + 12, 8), :]
            second = ref[chunk, pl.ds(16 * (n + 1) + 8, 8), :]
        pieces.append(jnp.where(low_half, first, second))
    return jnp.concatenate(pieces, axis=0)


def face_weight(velocity, face):
    normal = velocity[face // 2 : face // 2 + 1]
    return 6.0 * jnp.minimum(normal if face % 2 else -normal, 0.0)


def expand_faces(pair_rows, velocity, expansion):
    outer_parts, back_parts = [], []
    for pair in range(3):
        columns = jnp.transpose(pair_rows(pair))
        for side in range(2):
            weight = face_weight(velocity, 2 * pair + side) * (-STEP)
            outer_parts.append(columns[64 * side : 64 * side + 32] * weight)
            back_parts.append(columns[64 * side + 32 : 64 * side + 64] * STEP)
    terms = jnp.concatenate(
        [jnp.concatenate(outer_parts, axis=0), jnp.concatenate(back_parts, axis=0)], axis=1
    )
    high, low = split2(terms)
    added = jnp.dot(
        expansion, jnp.concatenate([high, low], axis=0), preferred_element_type=F32
    )
    return added[:, :128], added[:, 128:]


def exchange_kernel(
    n_dom,
    state_hbm,
    cotangent_hbm,
    velocity_hbm,
    dispersion_hbm,
    retained_hbm,
    kappa_hbm,
    block_hbm,
    source_hbm,
    send_hbm,
    forward_hbm,
    backward_hbm,
    expansion_hbm,
    advanced,
    adjoint,
    arrived_out,
    sums_out,
    outer_rows,
    velocity,
    send_rows,
    expansion,
    state,
    cotangent,
    dispersion,
    retained,
    block,
    forward_op,
    backward_op,
    kappa_ref,
    source_index,
    send_index,
    table,
    outgoing,
    kappa_rows,
    sums_row,
    sums_acc,
    in_sem,
    field_sem,
    index_sem,
    send_sem,
    recv_sem,
    kappa_send,
    kappa_recv,
    sums_send,
    sums_recv,
):
    dom = lax.axis_index("dom")
    sub = lax.axis_index("sub")
    loads = {}
    for number, (name, src, dst) in enumerate(
        [
            ("velocity", velocity_hbm, velocity),
            ("kappa", kappa_hbm, kappa_ref),
            ("block", block_hbm, block),
            ("dispersion", dispersion_hbm, dispersion),
            ("forward", forward_hbm, forward_op),
            ("backward", backward_hbm, backward_op),
            ("rows", send_hbm, send_rows),
            ("expansion", expansion_hbm, expansion),
        ]
    ):
        loads[name] = pltpu.make_async_copy(src, dst, in_sem.at[number])
    send_loads = [
        pltpu.make_async_copy(
            send_hbm.at[number], send_index.at[pl.ds(number * CAP, CAP)], index_sem.at[number]
        )
        for number in range(ROUNDS)
    ]
    source_loads = [
        pltpu.make_async_copy(
            source_hbm.at[face],
            source_index.at[pl.ds(face * ELEMS, ELEMS)],
            index_sem.at[ROUNDS + face],
        )
        for face in range(6)
    ]

    def field_load(number, chunk):
        src, dst = ((state_hbm, state), (cotangent_hbm, cotangent), (retained_hbm, retained))[number]
        start = chunk * 128 if isinstance(chunk, int) else pl.multiple_of(chunk * 128, 128)
        return pltpu.make_async_copy(
            src.at[:, pl.ds(start, 128)], dst.at[chunk], field_sem.at[number, chunk]
        )

    loads["velocity"].start()
    for number in range(2):
        field_load(number, 0).start()

    def dom_partner(offset):
        return dom + offset

    def has_partner(offset):
        return dom >= -offset if offset < 0 else dom < n_dom - offset

    def sub_partner(turn):
        return lax.rem(sub + turn, N_SUB)

    offsets = [n - REACH if n < REACH else n - REACH + 1 for n in range(ROUNDS)]
    barrier = pltpu.get_barrier_semaphore()
    partner_count = N_SUB - 1
    for offset in offsets:
        partner_count = partner_count + has_partner(offset).astype(jnp.int32)

        @pl.when(has_partner(offset))
        def _(offset=offset):
            pl.semaphore_signal(
                barrier, inc=1, device_id={"dom": dom_partner(offset)}, device_id_type=MESH
            )

    for turn in range(1, N_SUB):
        pl.semaphore_signal(
            barrier, inc=1, device_id={"sub": sub_partner(turn)}, device_id_type=MESH
        )

    for chunk in range(1, ELEMS // 128):
        for number in range(2):
            field_load(number, chunk).start()
    for load in send_loads:
        load.start()
    loads["kappa"].start()

    zero_tile = jnp.zeros((8, 128), F32)

    def clear(step, carry):
        table[pl.ds(pl.multiple_of(FACES + step * 8, 8), 8), :] = zero_tile
        return carry

    lax.fori_loop(0, (TABLE - FACES) // 8, clear, 0, unroll=17)

    loads["velocity"].wait()
    def build(chunk, carry):
        field_load(0, chunk).wait()
        field_load(1, chunk).wait()
        start = pl.multiple_of(chunk * 128, 128)
        cols = pl.ds(start, 128)
        speeds = velocity[:, cols]
        for face in range(6):
            both = [
                trace_of(state, face, chunk),
                trace_of(cotangent, face, chunk) * (-face_weight(speeds, face)),
            ]
            table[pl.ds(pl.multiple_of(face * ELEMS + start, 128), 128), :] = jnp.transpose(
                jnp.concatenate(both + both, axis=0)
            )
        return carry

    lax.fori_loop(0, ELEMS // 128, build, 0)
    low_row = iota((1, 128), 1) < 64

    for load in send_loads:
        load.wait()

    group = 32
    lane_row = iota((1, 128), 1)
    own_row = jnp.zeros((1, 128), F32)
    loads["kappa"].wait()
    for place in range(16):
        own_row = jnp.where(lane_row == sub * 16 + place, kappa_ref[place], own_row)
    kappa_rows[0] = own_row

    kappa_copies = [
        pltpu.make_async_remote_copy(
            src_ref=kappa_rows.at[0],
            dst_ref=kappa_rows.at[turn],
            send_sem=kappa_send.at[turn],
            recv_sem=kappa_recv.at[turn],
            device_id={"sub": sub_partner(turn)},
            device_id_type=MESH,
        )
        for turn in range(1, N_SUB)
    ]

    round_copies = []
    round_order = [(0, 0), (5, 0), (2, 0), (3, 0), (0, 1), (5, 1), (2, 1), (3, 1)]
    round_order += [(1, 0), (4, 0), (1, 1), (4, 1)]
    for turn, (number, half) in enumerate(round_order):

        def gather(step, carry, number=number):
            base = step * group
            values = []
            for place in range(group):
                first = send_index[number * CAP + base + place]
                second = send_index[number * CAP + HALF + base + place]
                values.append(
                    jnp.where(low_row, table[pl.ds(first, 1), :], table[pl.ds(second, 1), :])
                )
            for place in range(group):
                outgoing[number, pl.ds(base + place, 1), :] = values[place]
            return carry

        part = pl.ds(half * QUARTER, QUARTER)
        copy = pltpu.make_async_remote_copy(
            src_ref=outgoing.at[number, part],
            dst_ref=arrived_out.at[ROUNDS - 1 - number, part],
            send_sem=send_sem.at[number, half],
            recv_sem=recv_sem.at[ROUNDS - 1 - number, half],
            device_id={"dom": dom_partner(offsets[number])},
            device_id_type=MESH,
        )

        steps = QUARTER // group
        lax.fori_loop(half * steps, (half + 1) * steps, gather, 0)
        if turn == 0:
            pl.semaphore_wait(barrier, partner_count)
        pl.when(has_partner(offsets[number]))(copy.start)

        round_copies.append(copy)
        if turn == 3:
            for copy in kappa_copies:
                copy.start()
            loads["block"].start()
            for chunk in range(ELEMS // 128):
                field_load(2, chunk).start()
        if turn == 7:
            for load in source_loads:
                load.start()
            for name in ("dispersion", "forward", "backward", "rows", "expansion"):
                loads[name].start()

    width = 256
    sublane = iota((8, width), 0)

    def two_chunks(ref, chunk):
        return jnp.concatenate([ref[2 * chunk], ref[2 * chunk + 1]], axis=1)

    def free_sites(chunk):
        gain = jnp.where(iota((128, width), 0) < 64, 1.0, SECOND_SPECIES)
        return gain * (1.0 - two_chunks(retained, chunk))

    def block_hits(cols):
        return (iota((BLOCKS, width), 0) == block[:, cols]).astype(F32).astype(BF16)

    loads["block"].wait()
    for chunk in range(ELEMS // 128):
        field_load(2, chunk).wait()
    sums_acc[...] = jnp.zeros_like(sums_acc)

    def block_sums(chunk, carry):
        cols = pl.ds(pl.multiple_of(chunk * width, width), width)
        product = free_sites(chunk) * two_chunks(cotangent, chunk) * two_chunks(state, chunk)
        terms = jnp.sum(product, axis=0, keepdims=True)
        term_parts = jnp.concatenate(
            list(split3(terms)) + [jnp.zeros((13, width), BF16)], axis=0
        )
        sums_acc[...] += lax.dot_general(
            term_parts, block_hits(cols), (((1,), (1,)), ((), ())), preferred_element_type=F32
        )
        return carry

    lax.fori_loop(0, ELEMS // width, block_sums, 0)
    sums_row[...] = (sums_acc[0:1] + sums_acc[1:2]) + sums_acc[2:3]

    sums_out[0] = sums_row[...]
    sums_copies = [
        pltpu.make_async_remote_copy(
            src_ref=sums_row,
            dst_ref=sums_out.at[turn],
            send_sem=sums_send.at[turn],
            recv_sem=sums_recv.at[turn],
            device_id={"sub": sub_partner(turn)},
            device_id_type=MESH,
        )
        for turn in range(1, N_SUB)
    ]
    for copy in sums_copies:
        copy.start()

    for copy in kappa_copies:
        copy.wait_recv()
    slab = kappa_rows[0]
    for turn in range(1, N_SUB):
        slab = slab + kappa_rows[turn]
    slab_parts = jnp.concatenate(
        list(split3(slab)) + [jnp.zeros((13, 128), BF16)], axis=0
    )
    for name in ("dispersion", "forward", "backward", "rows", "expansion"):
        loads[name].wait()

    def volume(chunk, carry):
        start = pl.multiple_of(chunk * width, width)
        cols = pl.ds(start, width)
        rates = jnp.dot(slab_parts, block_hits(cols), preferred_element_type=F32)
        elem_rate = (rates[0:1] + rates[1:2]) + rates[2:3]
        speeds = velocity[:, cols]
        spread = dispersion[:, cols] * STEP

        field = two_chunks(state, chunk)
        dual = two_chunks(cotangent, chunk)
        weights = [face_weight(speeds, face) for face in range(6)]
        along_i = jnp.where(
            sublane % 4 == 0, weights[0], jnp.where(sublane % 4 == 3, weights[1], 0.0)
        )
        by_j = [
            along_i + jnp.where(sublane < 4, weights[2], 0.0),
            along_i + jnp.where(sublane >= 4, weights[3], 0.0),
        ]
        tiles = [by_j[0] + weights[4], by_j[1] + weights[4]]
        tiles += [by_j[0], by_j[1], by_j[0], by_j[1]]
        tiles += [by_j[0] + weights[5], by_j[1] + weights[5]]
        face_part = jnp.concatenate(tiles + tiles, axis=0)
        free = free_sites(chunk)
        factor = 1.0 + STEP * (face_part - elem_rate * free)
        for values, operator, target in (
            (field, forward_op, advanced),
            (dual, backward_op, adjoint),
        ):
            high, low = split2(values)
            images = jnp.dot(
                operator[...],
                jnp.concatenate([high, low, high], axis=0),
                preferred_element_type=F32,
            )
            target[:, cols] = (
                factor * values
                - (STEP * speeds[0:1]) * images[0:128]
                - (STEP * speeds[1:2]) * images[128:256]
                - (STEP * speeds[2:3]) * images[256:384]
                + spread * images[384:512]
            )
        return carry

    lax.fori_loop(0, ELEMS // width, volume, 0)
    for load in source_loads:
        load.wait()

    def pick(step, carry):
        base = step * (2 * group)
        values = [
            table[pl.ds(source_index[base + place], 1), :] for place in range(2 * group)
        ]
        for place in range(2 * group):
            outer_rows[pl.ds(base + place, 1), :] = values[place]
        return carry

    lax.fori_loop(0, FACES // (2 * group), pick, 0)

    for copy in kappa_copies:
        copy.wait_send()
    for copy in sums_copies:
        copy.wait()
    for (number, _), copy in zip(round_order, round_copies):
        pl.when(has_partner(offsets[number]))(copy.wait_send)
        pl.when(has_partner(offsets[ROUNDS - 1 - number]))(copy.wait_recv)


def merge_kernel(
    part_advanced,
    part_adjoint,
    arrived,
    sums,
    outer_rows,
    velocity,
    send_rows,
    expansion,
    advanced_out,
    adjoint_out,
    grad_out,
    spread,
    advanced,
    adjoint,
    send_index,
    rows,
    index_sem,
    out_sem,
):
    del outer_rows
    sub = lax.axis_index("sub")
    index_loads = [
        pltpu.make_async_copy(
            send_rows.at[number], send_index.at[pl.ds(number * CAP, CAP)], index_sem.at[number]
        )
        for number in range(ROUNDS)
    ]
    for load in index_loads:
        load.start()
    low_lanes = iota((HALF, 128), 1) < 64
    for number in range(ROUNDS):
        values = arrived[number]
        turned = pltpu.roll(values, 64, 1)
        rows[pl.ds(number * CAP, HALF), :] = jnp.where(low_lanes, values, turned)
        rows[pl.ds(number * CAP + HALF, HALF), :] = jnp.where(low_lanes, turned, values)
    for load in index_loads:
        load.wait()
    group = 384
    for number in range(ROUNDS):

        def scatter(step, carry, number=number):
            base = number * CAP + step * group
            values = [rows[pl.ds(base + place, 1), :] for place in range(group)]
            for place in range(group):
                spread[pl.ds(send_index[base + place], 1), :] = values[place]
            return carry

        lax.fori_loop(0, CAP // group, scatter, 0)
    total = jnp.zeros((1, 128), F32)
    for turn in range(N_SUB):
        total = total + sums[turn]
    total = pltpu.roll(total, 128 - sub * 16, 1)
    grad_out[...] = -STEP * total[:, :16]
    low_part = iota((128, 128), 1) < 64

    def results(chunk):
        cols = pl.ds(pl.multiple_of(chunk * 128, 128), 128)
        return [
            pltpu.make_async_copy(
                advanced.at[:, cols], advanced_out.at[:, cols], out_sem.at[0, chunk]
            ),
            pltpu.make_async_copy(
                adjoint.at[:, cols], adjoint_out.at[:, cols], out_sem.at[1, chunk]
            ),
        ]

    def close(chunk, carry):
        start = pl.multiple_of(chunk * 128, 128)
        cols = pl.ds(start, 128)

        def pair_rows(pair):
            first = spread[pl.ds(pl.multiple_of(2 * pair * ELEMS + start, 128), 128), :]
            second = spread[pl.ds(pl.multiple_of((2 * pair + 1) * ELEMS + start, 128), 128), :]
            return jnp.where(low_part, first, second)

        added = expand_faces(pair_rows, velocity[:, cols], expansion[...])
        advanced[:, cols] = part_advanced[:, cols] + added[0]
        adjoint[:, cols] = part_adjoint[:, cols] + added[1]
        for copy in results(chunk):
            copy.start()
        return carry

    lax.fori_loop(0, ELEMS // 128, close, 0, unroll=UNROLL_CLOSE)

    def finish(chunk, carry):
        for copy in results(chunk):
            copy.wait()
        return carry

    lax.fori_loop(0, ELEMS // 128, finish, 0)


def solution(mesh):
    n_dom = mesh.shape["dom"]
    matrices = nodal_matrices()
    forward_np = split_constant(matrices)
    backward_np = split_constant([matrix.T for matrix in matrices])
    expansion_np = face_expansion()
    in_hbm = pl.BlockSpec(memory_space=pltpu.HBM)
    in_vmem = pl.BlockSpec(memory_space=pltpu.VMEM)
    dma = pltpu.SemaphoreType.DMA
    field = jax.ShapeDtypeStruct((128, ELEMS), F32)

    def shards(
        state, cotangent, velocity, dispersion, retained, kappa, elem_block, face_source, send_face
    ):
        kept = functools.partial(pltpu.with_memory_space_constraint, memory_space=pltpu.HBM)
        forward_op = kept(jnp.asarray(forward_np))
        backward_op = kept(jnp.asarray(backward_np))
        expansion = kept(jnp.asarray(expansion_np))
        state, cotangent, velocity, retained = map(kept, (state, cotangent, velocity, retained))
        face_source, send_face, kappa = map(kept, (face_source, send_face, kappa))
        dispersion = kept(dispersion.reshape(1, ELEMS))
        elem_block = kept(elem_block.reshape(1, ELEMS))
        handed_on = pl.pallas_call(
            functools.partial(exchange_kernel, n_dom),
            out_shape=(
                field,
                field,
                jax.ShapeDtypeStruct((ROUNDS, HALF, 128), F32),
                jax.ShapeDtypeStruct((N_SUB, 1, 128), F32),
                jax.ShapeDtypeStruct((FACES + 8, 128), F32),
                jax.ShapeDtypeStruct((3, ELEMS), F32),
                jax.ShapeDtypeStruct((ROUNDS, CAP), jnp.int32),
                jax.ShapeDtypeStruct((128, 384), BF16),
            ),
            in_specs=[in_hbm] * 12,
            out_specs=(in_vmem,) * 8,
            scratch_shapes=[
                pltpu.VMEM((ELEMS // 128, 128, 128), F32),
                pltpu.VMEM((ELEMS // 128, 128, 128), F32),
                pltpu.VMEM((1, ELEMS), F32),
                pltpu.VMEM((ELEMS // 128, 128, 128), F32),
                pltpu.VMEM((1, ELEMS), jnp.int32),
                pltpu.VMEM((512, 384), BF16),
                pltpu.VMEM((512, 384), BF16),
                pltpu.SMEM((16,), F32),
                pltpu.SMEM((FACES,), jnp.int32),
                pltpu.SMEM((ROUNDS * CAP,), jnp.int32),
                pltpu.VMEM((TABLE, 128), F32),
                pltpu.VMEM((ROUNDS, HALF, 128), F32),
                pltpu.VMEM((N_SUB, 1, 128), F32),
                pltpu.VMEM((1, 128), F32),
                pltpu.VMEM((16, 128), F32),
                dma((9,)),
                dma((3, ELEMS // 128)),
                dma((ROUNDS + 6,)),
                dma((ROUNDS, 2)),
                dma((ROUNDS, 2)),
                dma((N_SUB,)),
                dma((N_SUB,)),
                dma((N_SUB,)),
                dma((N_SUB,)),
            ],
            compiler_params=pltpu.CompilerParams(
                collective_id=0, has_side_effects=True, vmem_limit_bytes=40 << 20
            ),
            name="exchange",
        )(
            state,
            cotangent,
            velocity,
            dispersion,
            retained,
            kappa,
            elem_block,
            face_source,
            send_face,
            forward_op,
            backward_op,
            expansion,
        )
        advanced, adjoint, grad, _ = pl.pallas_call(
            merge_kernel,
            out_shape=(
                field,
                field,
                jax.ShapeDtypeStruct((1, 16), F32),
                jax.ShapeDtypeStruct((FACES + 8, 128), F32),
            ),
            in_specs=[in_vmem] * 8,
            out_specs=(in_hbm, in_hbm, in_vmem, in_vmem),
            input_output_aliases={4: 3},
            scratch_shapes=[
                pltpu.VMEM((128, ELEMS), F32),
                pltpu.VMEM((128, ELEMS), F32),
                pltpu.SMEM((ROUNDS * CAP,), jnp.int32),
                pltpu.VMEM((ROUNDS * CAP, 128), F32),
                dma((ROUNDS,)),
                dma((2, ELEMS // 128)),
            ],
            compiler_params=pltpu.CompilerParams(vmem_limit_bytes=40 << 20),
            name="merge",
        )(*handed_on)
        return advanced, adjoint, grad.reshape(16)

    wide = P(None, ("dom", "sub"))
    flat = P(("dom", "sub"))
    return jax.shard_map(
        shards,
        mesh=mesh,
        in_specs=(wide, wide, wide, flat, wide, flat, flat, wide, wide),
        out_specs=(wide, wide, flat),
        check_vma=False,
    )
```
